32 devices in a mesh: gx: 4 (over z), gy: 2 (over y), gz: 4 (over x, core).
Axes of the slice: x: 2, y: 2, z: 4, core: 2. Of those that a mesh axis runs over, the one named last changes fastest.
Arguments:
- e_field: float32 [3, 32, 128, 256], P(None, 'gx', 'gz', 'gy'), may hold values from -6 to 6
- h_field: float32 [3, 32, 128, 256], P(None, 'gx', 'gz', 'gy'), may hold values from -6 to 6
- e_forward: float32 [3, 32, 128, 256], P(None, 'gx', 'gz', 'gy'), may hold values from -6 to 6
- e_coeff: float32 [32, 128, 256], P('gx', 'gz', 'gy'), may hold values from 0.1 to 0.5
- h_coeff: float32 [32, 128, 256], P('gx', 'gz', 'gy'), may hold values from 0.1 to 0.5
- dft_acc: float32 [16, 32, 128, 256], P(None, 'gx', 'gz', 'gy'), may hold values from -6 to 6
- design_mask: int32 [4, 4, 32], P('gx', 'gz', 'gy'), may hold values 0 or 1
- omega_t: float32 [8], replicated, may hold values from -3.140625 to 3.140625
- port_index: int32 [4], replicated, may hold values from 0 to 31
- port_owner: int32 [4], replicated, may hold values from 0 to 31
- port_modes: float32 [4, 2, 128, 256], P(None, None, 'gz', 'gy'), may hold values from -0.0234375 to 0.0234375
- monitor_acc: float32 [32, 16], P(('gx', 'gy', 'gz')), may hold values from -6 to 6
Outputs:
- e_next: float32 [3, 32, 128, 256], P(None, 'gx', 'gz', 'gy')
- h_next: float32 [3, 32, 128, 256], P(None, 'gx', 'gz', 'gy')
- dft_next: float32 [16, 32, 128, 256], P(None, 'gx', 'gz', 'gy')
- monitor_next: float32 [32, 16], P(('gx', 'gy', 'gz'))
The draws below stay inside these ranges and needn't reach their ends.
All inputs are finite; a program needn't handle non-finite values. No bound on the sum of `design_mask` on one device may be relied on, other than what follows from the above.
Results may differ from the reference program's by a relative error of at most 0.00011.
Values sent between devices are 32-bit elements; how exact they have to be, the bound alone decides.
A program may use at most 64 MiB of HBM per device.

```python
import math
import jax
import jax.numpy as jnp
from jax import lax

BX = 8
BY = 8
BZ = 32
NF = 8
NP = 4
NX = 32
NY = 256
NZ = 128
N_GX = 4
N_GY = 2
N_GZ = 4


def plant(array, key, low, top_value):
    extent = array.shape
    spot = [jax.random.randint(jax.random.fold_in(key, axis), (), 0, extent[axis]) for axis in range(len(extent))]
    array = array.at[tuple(spot)].set(low)
    longest = extent.index(max(extent))
    spot[longest] = (spot[longest] + 1) % extent[longest]
    return array.at[tuple(spot)].set(top_value)


def levels(key, shape, shards, least, high):
    def one(axis_at, shards_of):
        heights = jax.random.uniform(jax.random.fold_in(jax.random.fold_in(key, 6), axis_at), (shards_of,), jnp.float32, least / len(shards), high / len(shards))
        return jnp.repeat(jnp.exp(heights), shape[axis_at] // shards_of).reshape((-1,) + (1,) * (len(shape) - axis_at - 1))

    gain = one(*shards[0])
    for cut in shards[1:]:
        gain = gain * one(*cut)
    return gain


def normal_values(own_key, extent, width, limit, pieces=(), kind=jnp.bfloat16):
    array = width * jax.random.normal(own_key, extent, jnp.float32)
    if pieces:
        array = array * levels(own_key, extent, pieces, -0.22, 0.18)
    return jnp.clip(array, -limit, limit).astype(kind)


def setup_inputs(seed: int = 0) -> dict:
    key_of = jax.random.split(jax.random.key(seed), 13)
    return {
        "e_field": normal_values(key_of[0], (3, NX, NZ, NY), 1.0, 6.0, ((1, 4), (2, 4), (3, 2)), jnp.float32),
        "h_field": normal_values(key_of[1], (3, NX, NZ, NY), 1.0, 6.0, ((1, 4), (2, 4), (3, 2)), jnp.float32),
        "e_forward": normal_values(key_of[2], (3, NX, NZ, NY), 1.0, 6.0, ((1, 4), (2, 4), (3, 2)), jnp.float32),
        "e_coeff": jnp.clip(jnp.exp(math.log(0.5) - 1.609438 * jax.random.uniform(key_of[3], (NX, NZ, NY), jnp.float32) ** levels(key_of[3], (NX, NZ, NY), ((0, 4), (1, 4), (2, 2)), -0.2, 0.2)), 0.1, 0.5),
        "h_coeff": jnp.clip(jnp.exp(math.log(0.5) - 1.609438 * jax.random.uniform(key_of[4], (NX, NZ, NY), jnp.float32) ** levels(key_of[4], (NX, NZ, NY), ((0, 4), (1, 4), (2, 2)), -0.2, 0.2)), 0.1, 0.5),
        "dft_acc": normal_values(key_of[5], (2 * NF, NX, NZ, NY), 1.0, 6.0, ((1, 4), (2, 4), (3, 2)), jnp.float32),
        "design_mask": plant((jax.random.randint(key_of[6], (NX // BX, NZ // BZ, NY // BY), 0, 2) < 1).astype(jnp.int32), jax.random.fold_in(key_of[6], 1), 0, 1),
        "omega_t": jnp.clip(jax.random.uniform(key_of[7], (NF,), jnp.float32, -3.140625, 3.140625), -3.140625, 3.140625),
        "port_index": plant(jax.random.randint(key_of[8], (NP,), 0, NX), jax.random.fold_in(key_of[8], 1), 0, NX - 1).astype(jnp.int32),
        "port_owner": plant(jax.random.randint(key_of[9], (NP,), 0, N_GX * N_GY * N_GZ), jax.random.fold_in(key_of[9], 1), 0, (N_GX * N_GY * N_GZ) - 1).astype(jnp.int32),
        "port_modes": normal_values(key_of[10], (NP, 2, NZ, NY), (2 * NY * NZ) ** -0.5, 0.0234375, ((2, 4), (3, 2)), jnp.float32),
        "monitor_acc": normal_values(key_of[11], (N_GX * N_GY * N_GZ, 2 * NF), 1.0, 6.0, ((0, 32),), jnp.float32),
    }


def lower_diff(field, along):
    size = field.shape[along]
    before = jnp.concatenate([jnp.zeros_like(lax.slice_in_dim(field, 0, 1, axis=along)), lax.slice_in_dim(field, 0, size - 1, axis=along)], along)
    return field - before


def upper_diff(field, along):
    size = field.shape[along]
    after = jnp.concatenate([lax.slice_in_dim(field, 1, size, axis=along), jnp.zeros_like(lax.slice_in_dim(field, 0, 1, axis=along))], along)
    return after - field


def reference(e_field, h_field, e_forward, e_coeff, h_coeff, dft_acc, design_mask, omega_t, port_index, port_owner, port_modes, monitor_acc):
    curl_h = jnp.stack([
        lower_diff(h_field[2], 2) - lower_diff(h_field[1], 1),
        lower_diff(h_field[0], 1) - lower_diff(h_field[2], 0),
        lower_diff(h_field[1], 0) - lower_diff(h_field[0], 2)])
    e_next = e_field - e_coeff[None] * curl_h
    curl_e = jnp.stack([
        upper_diff(e_next[2], 2) - upper_diff(e_next[1], 1),
        upper_diff(e_next[0], 1) - upper_diff(e_next[2], 0),
        upper_diff(e_next[1], 0) - upper_diff(e_next[0], 2)])
    h_next = h_field + h_coeff[None] * curl_e
    weight = jnp.repeat(jnp.repeat(jnp.repeat(design_mask.astype(jnp.float32), BX, 0), BZ, 1), BY, 2)
    product = weight * jnp.sum(e_forward * e_next, axis=0)
    cosines = jnp.cos(omega_t)
    sines = jnp.sin(omega_t)
    phase = jnp.concatenate([cosines, -sines])
    dft_next = dft_acc + phase[:, None, None, None] * product[None]
    planes_y = e_next[1][port_index]
    planes_z = e_next[2][port_index]
    intersection = jnp.sum(port_modes[:, 0] * planes_y + port_modes[:, 1] * planes_z, axis=(1, 2))
    devices = monitor_acc.shape[0]
    owned = (port_owner[None, :] == jnp.arange(devices, dtype=jnp.int32)[:, None]).astype(jnp.float32)
    monitor_next = monitor_acc + jnp.dot(owned, intersection[:, None] * phase[None, :], precision=lax.Precision.HIGHEST)
    return e_next, h_next, dft_next, monitor_next
```

```python
import functools

import jax
import jax.numpy as jnp
from jax import lax
from jax.experimental import pallas as pl
from jax.experimental.pallas import tpu as pltpu
from jax.sharding import PartitionSpec as P

BY = 8
NF = 8
NP = 4
UNROLL = 32


def tiles(plane):
    return [plane[8 * q : 8 * q + 8] for q in range(plane.shape[0] // 8)]


def pack_lane(fields, lane_of, lane):
    packed = jnp.zeros((8, 128), jnp.float32)
    k = 0
    for plane in fields:
        for tile in tiles(plane):
            moved = pltpu.roll(tile, (k - lane_of) % 128, 1)
            packed = jnp.where(lane == k, moved, packed)
            k += 1
    return packed


def unpack_lane(packed, first, count, lane_of, keep):
    out = [pltpu.roll(packed, (lane_of - first - q) % 128, 1) for q in range(count)]
    return jnp.where(keep, jnp.concatenate(out, 0), 0.0)


def step(
    sizes, e_hbm, h_hbm, ef_hbm, ec_hbm, hc_hbm, dft_hbm, modes_hbm,
    mask_hbm, omega_hbm, pidx_hbm, powner_hbm, mon_hbm,
    en, hn, dn, mon_out,
    ef, ec, hc, modes, mask_ref, omega_ref, pidx_ref, powner_ref, mon_ref,
    hx_in, hy_in, hz_in, ex_in, ey_in, ez_in, hy_out, ey_out, mine, rows,
    cx_in, cy_in, cz_in, cy_out, cz_out,
    load_sems, h_send, h_recv, e_send, e_recv, c_send, c_recv, all_send, all_recv, known_sems,
):
    n_gx, n_gy, n_gz = sizes
    n = n_gx * n_gy * n_gz
    a, b, c = lax.axis_index("gx"), lax.axis_index("gy"), lax.axis_index("gz")
    stride_x, stride_y = n_gy * n_gz, n_gz
    me = a * stride_x + b * stride_y + c
    nx, nz, ny = ec.shape
    zt = nz // 8

    lines = [(a, n_gx, stride_x), (b, n_gy, stride_y), (c, n_gz, 1)]
    partners = [
        [me + (lax.rem(at + k, size) - at) * stride for k in range(1, size)]
        for at, size, stride in lines
    ]

    barrier = pltpu.get_barrier_semaphore()
    loads = [
        pltpu.make_async_copy(src, dst, load_sems.at[i])
        for i, (src, dst) in enumerate(
            [(h_hbm, hn), (e_hbm, en), (ec_hbm, ec), (modes_hbm, modes), (hc_hbm, hc), (ef_hbm, ef), (dft_hbm, dn),
             (mask_hbm, mask_ref), (omega_hbm, omega_ref), (pidx_hbm, pidx_ref), (powner_hbm, powner_ref), (mon_hbm, mon_ref)]
        )
    ]
    for i in (9, 2, 3, 0, 1):
        loads[i].start()
    for line in partners:
        for dev in line:
            pl.semaphore_signal(
                barrier, inc=1, device_id=dev, device_id_type=pl.DeviceIdType.LOGICAL
            )
    for i in (7, 8, 10, 11, 4, 5, 6):
        loads[i].start()

    def remote(src, dst, send, recv, dev):
        return pltpu.make_async_remote_copy(
            src_ref=src, dst_ref=dst, send_sem=send, recv_sem=recv,
            device_id=dev, device_id_type=pl.DeviceIdType.LOGICAL,
        )

    up = [(a < n_gx - 1, stride_x), (b < n_gy - 1, stride_y), (c < n_gz - 1, 1)]
    down = [(a > 0, stride_x), (b > 0, stride_y), (c > 0, 1)]
    h_copies = [
        remote(src, dst, h_send.at[i], h_recv.at[i], jnp.where(up[i][0], me + up[i][1], 0))
        for i, (src, dst) in enumerate(
            [(hn.at[1:3, nx - 1], hx_in), (hy_out, hy_in), (hn.at[0:2, :, nz - 1], hz_in)]
        )
    ]
    e_copies = [
        remote(src, dst, e_send.at[i], e_recv.at[i], jnp.where(down[i][0], me - down[i][1], 0))
        for i, (src, dst) in enumerate(
            [(en.at[1:3, 0], ex_in), (ey_out, ey_in), (en.at[0:2, :, 0], ez_in)]
        )
    ]

    c_copies = [
        remote(src, dst, c_send.at[i], c_recv.at[i], jnp.where(down[i][0], me - down[i][1], 0))
        for i, (src, dst) in enumerate([(ec.at[0], cx_in), (cy_out, cy_in), (cz_out, cz_in)])
    ]

    row = lax.broadcasted_iota(jnp.int32, (nz, ny), 0)
    lane = lax.broadcasted_iota(jnp.int32, (nz, ny), 1)
    lane8 = lax.broadcasted_iota(jnp.int32, (8, 128), 1)

    sub8 = lax.broadcasted_iota(jnp.int32, (8, 128), 0)

    def tell(line, sem):
        for dev in line:
            pl.semaphore_signal(
                sem, inc=1, device_id=dev, device_id_type=pl.DeviceIdType.LOGICAL
            )

    for i in (9, 2, 3):
        loads[i].wait()
    ports = []
    for p in range(NP):
        x_of = pidx_ref[p] - a * nx
        ports.append(((x_of >= 0) & (x_of < nx), x_of == nx, jnp.clip(x_of, 0, nx - 1)))
    cy_out[...] = pack_lane(
        [modes[p, 1] * ec[at] for p, (_, _, at) in enumerate(ports)], 0, lane8
    )
    for p, (_, _, at) in enumerate(ports):
        cz_out[p : p + 1] = modes[p, 0, 0:1] * ec[at, 0:1]

    pl.semaphore_wait(barrier, sum(map(len, partners)))
    for i in (1, 0, 2):
        pl.when(down[i][0])(c_copies[i].start)
    tell(partners[1], known_sems.at[0])

    loads[0].wait()
    hy_out[...] = pack_lane(
        [hn[comp, x] for comp in (0, 2) for x in range(nx)], ny - 1, lane8
    )
    for i in (0, 2, 1):
        pl.when(up[i][0])(h_copies[i].start)

    for i in (7, 8, 10, 11):
        loads[i].wait()
    angle_rows = jnp.zeros((8, 128), jnp.float32)
    angle_lanes = jnp.zeros((8, 128), jnp.float32)
    for f in range(NF):
        angle_rows = jnp.where(sub8 == f, omega_ref[f], angle_rows)
        angle_lanes = jnp.where((lane8 == f) | (lane8 == f + NF), omega_ref[f], angle_lanes)
    cosines, sines = jnp.cos(angle_rows), -jnp.sin(angle_rows)
    phase_lanes = jnp.where(lane8 < NF, jnp.cos(angle_lanes), -jnp.sin(angle_lanes))
    weight = jnp.zeros((8, 128), jnp.float32)
    for k in range(ny // BY):
        weight = jnp.where(lane8 // BY == k, mask_ref[0, 0, k].astype(jnp.float32), weight)
    weight = jnp.concatenate([weight] * zt, 0)

    loads[1].wait()

    def low(plane, axis):
        first = (row if axis == 0 else lane) == 0
        return plane - jnp.where(first, 0.0, pltpu.roll(plane, 1, axis))

    for x in range(nx):
        h0, h1, h2 = hn[0, x], hn[1, x], hn[2, x]
        d1 = h1 - hn[1, x - 1] if x else h1
        d2 = h2 - hn[2, x - 1] if x else h2
        coef = ec[x]
        en[0, x] = en[0, x] - coef * (low(h2, 1) - low(h1, 0))
        en[1, x] = en[1, x] - coef * (low(h0, 0) - d2)
        en[2, x] = en[2, x] - coef * (d1 - low(h0, 1))

    if n_gy > 1:
        pl.semaphore_wait(known_sems.at[0], n_gy - 1)
    tell(partners[2], known_sems.at[1])

    h_packed = pack_lane([hn[0, at] for _, _, at in ports], ny - 1, lane8)
    partial = []
    for p, (inside, _, at) in enumerate(ports):
        both = modes[p, 0] * en[1, at] + modes[p, 1] * en[2, at]
        partial.append(jnp.where(inside, functools.reduce(jnp.add, tiles(both)), 0.0))

    for i, landing in enumerate((cx_in, cy_in, cz_in)):
        pl.when(up[i][0])(c_copies[i].wait_recv)

        @pl.when(jnp.logical_not(up[i][0]))
        def _(landing=landing):
            landing[...] = jnp.zeros_like(landing)

    y_part = h_packed * cy_in[...]
    for p, (inside, above, at) in enumerate(ports):
        x_part = cx_in[...] * (modes[p, 1] * hn[1, nx - 1] - modes[p, 0] * hn[2, nx - 1])
        x_part = jnp.where(above, functools.reduce(jnp.add, tiles(x_part)), 0.0)
        yz_part = jnp.where(sub8 == 0, cz_in[p : p + 1] * hn[0, at, nz - 1 : nz], 0.0)
        yz_part = yz_part - jnp.where(lane8 // zt == p, y_part, 0.0)
        total = partial[p] + x_part + jnp.where(inside, yz_part, 0.0)
        mine[p : p + 1] = jnp.sum(total, axis=0, keepdims=True)

    if n_gz > 1:
        pl.semaphore_wait(known_sems.at[1], n_gz - 1)

    def send_row(k, _):
        remote(mine, rows.at[k - 1], all_send, all_recv, lax.rem(me + k, n)).start()
        return 0

    lax.fori_loop(1, n, send_row, 0, unroll=n <= UNROLL)

    for i, landing in enumerate((hx_in, hy_in, hz_in)):
        pl.when(down[i][0])(h_copies[i].wait_recv)

        @pl.when(jnp.logical_not(down[i][0]))
        def _(landing=landing):
            landing[...] = jnp.zeros_like(landing)

    packed = hy_in[...]
    for x in range(nx):
        coef = ec[x]
        y0 = unpack_lane(packed, x * zt, zt, 0, lane == 0)
        y2 = unpack_lane(packed, (nx + x) * zt, zt, 0, lane == 0)
        z0 = jnp.where(sub8 == 0, hz_in[0, x : x + 1, :], 0.0)
        z1 = jnp.where(sub8 == 0, hz_in[1, x : x + 1, :], 0.0)
        rest = jnp.zeros((nz - 8, ny), jnp.float32)
        z0, z1 = jnp.concatenate([z0, rest], 0), jnp.concatenate([z1, rest], 0)
        add0, add1, add2 = y2 - z1, z0, -y0
        if x == 0:
            add1 = add1 - hx_in[1]
            add2 = add2 + hx_in[0]
        en[0, x] = en[0, x] + coef * add0
        en[1, x] = en[1, x] + coef * add1
        en[2, x] = en[2, x] + coef * add2

    for i in (0, 2):
        pl.when(down[i][0])(e_copies[i].start)
    ey_out[...] = pack_lane([en[comp, x] for comp in (0, 2) for x in range(nx)], 0, lane8)
    pl.when(down[1][0])(e_copies[1].start)

    for i in range(3):
        pl.when(up[i][0])(h_copies[i].wait_send)
    loads[4].wait()

    def high(plane, axis):
        last = (row == nz - 1) if axis == 0 else (lane == ny - 1)
        return jnp.where(last, 0.0, pltpu.roll(plane, plane.shape[axis] - 1, axis)) - plane

    for x in range(nx):
        e0, e1, e2 = en[0, x], en[1, x], en[2, x]
        d1 = en[1, x + 1] - e1 if x < nx - 1 else -e1
        d2 = en[2, x + 1] - e2 if x < nx - 1 else -e2
        coef = hc[x]
        hn[0, x] = hn[0, x] + coef * (high(e2, 1) - high(e1, 0))
        hn[1, x] = hn[1, x] + coef * (high(e0, 0) - d2)
        hn[2, x] = hn[2, x] + coef * (d1 - high(e0, 1))

    loads[5].wait()
    loads[6].wait()
    for x in range(nx):
        product = weight * (ef[0, x] * en[0, x] + ef[1, x] * en[1, x] + ef[2, x] * en[2, x])
        for f in range(NF):
            dn[f, x] = dn[f, x] + cosines[f : f + 1] * product
            dn[NF + f, x] = dn[NF + f, x] + sines[f : f + 1] * product

    for i, landing in enumerate((ex_in, ey_in, ez_in)):
        pl.when(up[i][0])(e_copies[i].wait_recv)

        @pl.when(jnp.logical_not(up[i][0]))
        def _(landing=landing):
            landing[...] = jnp.zeros_like(landing)

    packed = ey_in[...]
    for x in range(nx):
        coef = hc[x]
        y0 = unpack_lane(packed, x * zt, zt, ny - 1, lane == ny - 1)
        y2 = unpack_lane(packed, (nx + x) * zt, zt, ny - 1, lane == ny - 1)
        z0 = jnp.where(sub8 == 7, ez_in[0, x : x + 1, :], 0.0)
        z1 = jnp.where(sub8 == 7, ez_in[1, x : x + 1, :], 0.0)
        rest = jnp.zeros((nz - 8, ny), jnp.float32)
        z0, z1 = jnp.concatenate([rest, z0], 0), jnp.concatenate([rest, z1], 0)
        add0, add1, add2 = y2 - z1, z0, -y0
        if x == nx - 1:
            add1 = add1 - ex_in[1]
            add2 = add2 + ex_in[0]
        hn[0, x] = hn[0, x] + coef * add0
        hn[1, x] = hn[1, x] + coef * add1
        hn[2, x] = hn[2, x] + coef * add2
    for i in range(3):
        pl.when(down[i][0])(e_copies[i].wait_send)
        pl.when(down[i][0])(c_copies[i].wait_send)

    remote(rows, rows, all_send, all_recv, me).wait()
    intersection = jnp.sum(rows[...], axis=0) + mine[...]
    port = lax.broadcasted_iota(jnp.int32, (NP, 128), 0)
    owned = jnp.zeros((NP, 128), jnp.float32)
    for p in range(NP):
        owned = jnp.where(port == p, (powner_ref[p] == me).astype(jnp.float32), owned)
    total = jnp.sum(owned * intersection, axis=0, keepdims=True)
    total = jnp.sum(total, axis=1, keepdims=True)
    mon_out[...] = mon_ref[...] + total * phase_lanes[0:1, : 2 * NF]


def write_out(en, hn, dn, mon, en_out, hn_out, dn_out, mon_out, sems):
    parts = 4
    size = dn.shape[0] // parts
    pairs = [(dn.at[pl.ds(i * size, size)], dn_out.at[pl.ds(i * size, size)]) for i in range(parts)]
    pairs += [(en, en_out), (hn, hn_out), (mon, mon_out)]
    copies = [pltpu.make_async_copy(src, dst, sems.at[i]) for i, (src, dst) in enumerate(pairs)]
    for copy in copies:
        copy.start()
    for copy in copies:
        copy.wait()


def body(sizes, e_field, h_field, e_forward, e_coeff, h_coeff, dft_acc, design_mask,
         omega_t, port_index, port_owner, port_modes, monitor_acc):
    nx, nz, ny = e_coeff.shape
    n = sizes[0] * sizes[1] * sizes[2]
    f32 = jnp.float32
    hbm = pl.BlockSpec(memory_space=pltpu.HBM)
    vmem = pl.BlockSpec(memory_space=pltpu.VMEM)
    far = lambda x: pltpu.with_memory_space_constraint(x, pltpu.HBM)
    held = pl.pallas_call(
        functools.partial(step, sizes),
        out_shape=[
            pltpu.VMEM(e_field.shape, f32),
            pltpu.VMEM(h_field.shape, f32),
            pltpu.VMEM(dft_acc.shape, f32),
            pltpu.VMEM(monitor_acc.shape, f32),
        ],
        in_specs=[hbm] * 12,
        out_specs=[vmem] * 4,
        scratch_shapes=[
            pltpu.VMEM(e_forward.shape, f32),
            pltpu.VMEM(e_coeff.shape, f32),
            pltpu.VMEM(h_coeff.shape, f32),
            pltpu.VMEM(port_modes.shape, f32),
            pltpu.SMEM(design_mask.shape, jnp.int32),
            pltpu.SMEM(omega_t.shape, f32),
            pltpu.SMEM(port_index.shape, jnp.int32),
            pltpu.SMEM(port_owner.shape, jnp.int32),
            pltpu.VMEM(monitor_acc.shape, f32),
            pltpu.VMEM((2, nz, ny), f32),
            pltpu.VMEM((8, 128), f32),
            pltpu.VMEM((2, nx, ny), f32),
            pltpu.VMEM((2, nz, ny), f32),
            pltpu.VMEM((8, 128), f32),
            pltpu.VMEM((2, nx, ny), f32),
            pltpu.VMEM((8, 128), f32),
            pltpu.VMEM((8, 128), f32),
            pltpu.VMEM((NP, 128), f32),
            pltpu.VMEM((n - 1, NP, 128), f32),
            pltpu.VMEM((nz, ny), f32),
            pltpu.VMEM((8, 128), f32),
            pltpu.VMEM((NP, 128), f32),
            pltpu.VMEM((8, 128), f32),
            pltpu.VMEM((NP, 128), f32),
            pltpu.SemaphoreType.DMA((12,)),
            pltpu.SemaphoreType.DMA((3,)),
            pltpu.SemaphoreType.DMA((3,)),
            pltpu.SemaphoreType.DMA((3,)),
            pltpu.SemaphoreType.DMA((3,)),
            pltpu.SemaphoreType.DMA((3,)),
            pltpu.SemaphoreType.DMA((3,)),
            pltpu.SemaphoreType.DMA,
            pltpu.SemaphoreType.DMA,
            pltpu.SemaphoreType.REGULAR((2,)),
        ],
        compiler_params=pltpu.CompilerParams(
            collective_id=0, has_side_effects=True, vmem_limit_bytes=24 * 2**20
        ),
        name="yee_step",
    )(*map(far, (e_field, h_field, e_forward, e_coeff, h_coeff, dft_acc, port_modes,
      design_mask, omega_t, port_index, port_owner, monitor_acc)))
    shape = lambda x: jax.ShapeDtypeStruct(x.shape, f32)
    return pl.pallas_call(
        write_out,
        out_shape=[shape(x) for x in (e_field, h_field, dft_acc, monitor_acc)],
        in_specs=[vmem] * 4,
        out_specs=[hbm] * 4,
        scratch_shapes=[pltpu.SemaphoreType.DMA((7,))],
        name="write_out",
    )(*[pltpu.with_memory_space_constraint(x, pltpu.VMEM) for x in held])


def solution(mesh):
    grid = P(None, "gx", "gz", "gy")
    brick = P("gx", "gz", "gy")
    own = P(("gx", "gy", "gz"), None)
    sizes = tuple(mesh.shape[axis] for axis in ("gx", "gy", "gz"))
    in_specs = (grid, grid, grid, brick, brick, grid, brick, P(), P(), P(),
                P(None, None, "gz", "gy"), own)
    return jax.shard_map(
        functools.partial(body, sizes), mesh=mesh, in_specs=in_specs,
        out_specs=(grid, grid, grid, own), check_vma=False,
    )
```

```python
import functools

import jax
import jax.numpy as jnp
from jax import lax
from jax.experimental import pallas as pl
from jax.experimental.pallas import tpu as pltpu
from jax.sharding import PartitionSpec as P

BY = 8
NF = 8
NP = 4
UNROLL = 32


def tiles(plane):
    return [plane[8 * q : 8 * q + 8] for q in range(plane.shape[0] // 8)]


def pack_lane(fields, lane_of, lane):
    packed = jnp.zeros((8, 128), jnp.float32)
    k = 0
    for plane in fields:
        for tile in tiles(plane):
            moved = pltpu.roll(tile, (k - lane_of) % 128, 1)
            packed = jnp.where(lane == k, moved, packed)
            k += 1
    return packed


def unpack_lane(packed, first, count, lane_of, keep):
    out = [pltpu.roll(packed, (lane_of - first - q) % 128, 1) for q in range(count)]
    return jnp.where(keep, jnp.concatenate(out, 0), 0.0)


def step(
    sizes, e_hbm, h_hbm, ef_hbm, ec_hbm, hc_hbm, dft_hbm, modes_hbm,
    mask_hbm, omega_hbm, pidx_hbm, powner_hbm, mon_hbm,
    en, hn, dn, mon_out,
    ef, ec, hc, modes, mask_ref, omega_ref, pidx_ref, powner_ref, mon_ref,
    hx_in, hy_in, hz_in, ex_in, ey_in, ez_in, hy_out, ey_out, mine, rows,
    cx_in, cz_in, mz_in,
    load_sems, h_send, h_recv, e_send, e_recv, c_send, c_recv, all_send, all_recv, known_sems,
):
    n_gx, n_gy, n_gz = sizes
    n = n_gx * n_gy * n_gz
    kinds = rows.shape[1]
    a, b, c = lax.axis_index("gx"), lax.axis_index("gy"), lax.axis_index("gz")
    stride_x, stride_y = n_gy * n_gz, n_gz
    me = a * stride_x + b * stride_y + c
    nx, nz, ny = ec.shape
    zt = nz // 8

    lines = [(a, n_gx, stride_x), (b, n_gy, stride_y), (c, n_gz, 1)]
    partners = [
        [me + (lax.rem(at + k, size) - at) * stride for k in range(1, size)]
        for at, size, stride in lines
    ]

    barrier = pltpu.get_barrier_semaphore()
    loads = [
        pltpu.make_async_copy(src, dst, load_sems.at[i])
        for i, (src, dst) in enumerate(
            [(h_hbm, hn), (e_hbm, en), (ec_hbm, ec), (modes_hbm, modes), (hc_hbm, hc), (ef_hbm, ef), (dft_hbm, dn),
             (mask_hbm, mask_ref), (omega_hbm, omega_ref), (pidx_hbm, pidx_ref), (powner_hbm, powner_ref), (mon_hbm, mon_ref)]
        )
    ]
    for i in (9, 2, 3, 0, 1):
        loads[i].start()
    for line in partners:
        for dev in line:
            pl.semaphore_signal(
                barrier, inc=1, device_id=dev, device_id_type=pl.DeviceIdType.LOGICAL
            )
    for i in (7, 8, 10, 11, 4, 5, 6):
        loads[i].start()

    def remote(src, dst, send, recv, dev):
        return pltpu.make_async_remote_copy(
            src_ref=src, dst_ref=dst, send_sem=send, recv_sem=recv,
            device_id=dev, device_id_type=pl.DeviceIdType.LOGICAL,
        )

    up = [(a < n_gx - 1, stride_x), (b < n_gy - 1, stride_y), (c < n_gz - 1, 1)]
    down = [(a > 0, stride_x), (b > 0, stride_y), (c > 0, 1)]
    h_copies = [
        remote(src, dst, h_send.at[i], h_recv.at[i], jnp.where(up[i][0], me + up[i][1], 0))
        for i, (src, dst) in enumerate(
            [(hn.at[1:3, nx - 1], hx_in), (hy_out, hy_in), (hn.at[0:2, :, nz - 1], hz_in)]
        )
    ]
    e_copies = [
        remote(src, dst, e_send.at[i], e_recv.at[i], jnp.where(down[i][0], me - down[i][1], 0))
        for i, (src, dst) in enumerate(
            [(en.at[1:3, 0], ex_in), (ey_out, ey_in), (en.at[0:2, :, 0], ez_in)]
        )
    ]

    c_copies = [
        (i, remote(src, dst, c_send.at[k], c_recv.at[k], jnp.where(down[i][0], me - down[i][1], 0)))
        for k, (i, src, dst) in enumerate(
            [(0, ec_hbm.at[0], cx_in), (2, ec_hbm.at[:, 0], cz_in), (2, modes_hbm.at[:, 0, 0], mz_in)]
        )
    ]

    row = lax.broadcasted_iota(jnp.int32, (nz, ny), 0)
    lane = lax.broadcasted_iota(jnp.int32, (nz, ny), 1)
    lane8 = lax.broadcasted_iota(jnp.int32, (8, 128), 1)
    group = 128 // NP

    sub8 = lax.broadcasted_iota(jnp.int32, (8, 128), 0)

    def tell(line, sem):
        for dev in line:
            pl.semaphore_signal(
                sem, inc=1, device_id=dev, device_id_type=pl.DeviceIdType.LOGICAL
            )

    pl.semaphore_wait(barrier, sum(map(len, partners)))
    for i, copy in c_copies:
        pl.when(down[i][0])(copy.start)
    tell(partners[1], known_sems.at[0])

    loads[0].wait()
    hy_out[...] = pack_lane(
        [hn[comp, x] for comp in (0, 2) for x in range(nx)], ny - 1, lane8
    )
    for i in (0, 2, 1):
        pl.when(up[i][0])(h_copies[i].start)

    for i in (7, 8, 9, 10, 11):
        loads[i].wait()
    angle_rows = jnp.zeros((8, 128), jnp.float32)
    angle_lanes = jnp.zeros((8, 128), jnp.float32)
    for f in range(NF):
        angle_rows = jnp.where(sub8 == f, omega_ref[f], angle_rows)
        angle_lanes = jnp.where((lane8 == f) | (lane8 == f + NF), omega_ref[f], angle_lanes)
    cosines, sines = jnp.cos(angle_rows), -jnp.sin(angle_rows)
    phase_lanes = jnp.where(lane8 < NF, jnp.cos(angle_lanes), -jnp.sin(angle_lanes))
    weight = jnp.zeros((8, 128), jnp.float32)
    for k in range(ny // BY):
        weight = jnp.where(lane8 // BY == k, mask_ref[0, 0, k].astype(jnp.float32), weight)
    weight = jnp.concatenate([weight] * zt, 0)

    for i in (1, 2, 3):
        loads[i].wait()

    ports = []
    for p in range(NP):
        x_of = pidx_ref[p] - a * nx
        ports.append(((x_of >= 0) & (x_of < nx), x_of == nx, jnp.clip(x_of, 0, nx - 1)))

    def low(plane, axis):
        first = (row if axis == 0 else lane) == 0
        return plane - jnp.where(first, 0.0, pltpu.roll(plane, 1, axis))

    for x in range(nx):
        h0, h1, h2 = hn[0, x], hn[1, x], hn[2, x]
        d1 = h1 - hn[1, x - 1] if x else h1
        d2 = h2 - hn[2, x - 1] if x else h2
        coef = ec[x]
        en[0, x] = en[0, x] - coef * (low(h2, 1) - low(h1, 0))
        en[1, x] = en[1, x] - coef * (low(h0, 0) - d2)
        en[2, x] = en[2, x] - coef * (d1 - low(h0, 1))

    if n_gy > 1:
        pl.semaphore_wait(known_sems.at[0], n_gy - 1)
    tell(partners[2], known_sems.at[1])

    partial = []
    for p, (inside, _, at) in enumerate(ports):
        both = modes[p, 0] * en[1, at] + modes[p, 1] * en[2, at]
        partial.append(jnp.where(inside, functools.reduce(jnp.add, tiles(both)), 0.0))

    def column(planes, lane_of):
        packed = jnp.zeros((8, 128), jnp.float32)
        for p, plane in enumerate(planes):
            for q, tile in enumerate(tiles(plane)):
                to = p * group + q
                packed = jnp.where(lane8 == to, pltpu.roll(tile, (to - lane_of) % 128, 1), packed)
        packed = pltpu.roll(packed, 0, 1, stride=zt, stride_axis=0)
        return jnp.sum(packed, axis=0, keepdims=True)

    columns = []
    if n_gy > 1:
        below = [jnp.where(inside, -hn[0, at], 0.0) for inside, _, at in ports]
        above = [modes[p, 1] * ec[at] for p, (_, _, at) in enumerate(ports)]
        if n_gy == 2:
            edge = jnp.broadcast_to(b == 0, (nz, ny))
            both = [jnp.where(edge, pltpu.roll(u, 1, 1), v) for u, v in zip(below, above)]
            columns = [column(both, 0)]
        else:
            columns = [column(below, ny - 1), column(above, 0)]

    x_parts = [
        jnp.where(over, modes[p, 1] * hn[1, nx - 1] - modes[p, 0] * hn[2, nx - 1], 0.0)
        for p, (_, over, _) in enumerate(ports)
    ]
    z_parts = [jnp.where(inside, hn[0, at, nz - 1 : nz], 0.0) for inside, _, at in ports]

    for (i, copy), landing in zip(c_copies, (cx_in, cz_in, mz_in)):
        pl.when(up[i][0])(copy.wait_recv)

        @pl.when(jnp.logical_not(up[i][0]))
        def _(landing=landing):
            landing[...] = jnp.zeros_like(landing)

    share = jnp.zeros((8, 128), jnp.float32)
    for p, (_, _, at) in enumerate(ports):
        x_part = functools.reduce(jnp.add, tiles(cx_in[...] * x_parts[p]))
        z_part = mz_in[p : p + 1] * cz_in[pl.ds(at, 1)] * z_parts[p]
        total = partial[p] + x_part + jnp.where(sub8 == 0, z_part, 0.0)
        width = 128
        while width > group:
            width //= 2
            total = total + pltpu.roll(total, width, 1)
        share = jnp.where(lane8 // group == p, total, share)
    mine[0, 0:1] = jnp.sum(share, axis=0, keepdims=True)
    for k, vector in enumerate(columns):
        mine[0, k + 1 : k + 2] = vector
    rows[pl.ds(me, 1)] = mine[...]

    if n_gz > 1:
        pl.semaphore_wait(known_sems.at[1], n_gz - 1)

    def send_row(k, _):
        to = k + jnp.where(k >= me, 1, 0)
        remote(mine.at[0], rows.at[me], all_send, all_recv, to).start()
        return 0

    lax.fori_loop(0, n - 1, send_row, 0, unroll=n <= UNROLL)

    for i, landing in enumerate((hx_in, hy_in, hz_in)):
        pl.when(down[i][0])(h_copies[i].wait_recv)

        @pl.when(jnp.logical_not(down[i][0]))
        def _(landing=landing):
            landing[...] = jnp.zeros_like(landing)

    packed = hy_in[...]
    for x in range(nx):
        coef = ec[x]
        y0 = unpack_lane(packed, x * zt, zt, 0, lane == 0)
        y2 = unpack_lane(packed, (nx + x) * zt, zt, 0, lane == 0)
        z0 = jnp.where(sub8 == 0, hz_in[0, x : x + 1, :], 0.0)
        z1 = jnp.where(sub8 == 0, hz_in[1, x : x + 1, :], 0.0)
        rest = jnp.zeros((nz - 8, ny), jnp.float32)
        z0, z1 = jnp.concatenate([z0, rest], 0), jnp.concatenate([z1, rest], 0)
        add0, add1, add2 = y2 - z1, z0, -y0
        if x == 0:
            add1 = add1 - hx_in[1]
            add2 = add2 + hx_in[0]
        en[0, x] = en[0, x] + coef * add0
        en[1, x] = en[1, x] + coef * add1
        en[2, x] = en[2, x] + coef * add2
        if x == 0:
            pl.when(down[0][0])(e_copies[0].start)

    pl.when(down[2][0])(e_copies[2].start)
    ey_out[...] = pack_lane([en[comp, x] for comp in (0, 2) for x in range(nx)], 0, lane8)
    pl.when(down[1][0])(e_copies[1].start)

    for i in range(3):
        pl.when(up[i][0])(h_copies[i].wait_send)
    loads[4].wait()

    def high(plane, axis):
        last = (row == nz - 1) if axis == 0 else (lane == ny - 1)
        return jnp.where(last, 0.0, pltpu.roll(plane, plane.shape[axis] - 1, axis)) - plane

    for x in range(nx):
        e0, e1, e2 = en[0, x], en[1, x], en[2, x]
        d1 = en[1, x + 1] - e1 if x < nx - 1 else -e1
        d2 = en[2, x + 1] - e2 if x < nx - 1 else -e2
        coef = hc[x]
        hn[0, x] = hn[0, x] + coef * (high(e2, 1) - high(e1, 0))
        hn[1, x] = hn[1, x] + coef * (high(e0, 0) - d2)
        hn[2, x] = hn[2, x] + coef * (d1 - high(e0, 1))

    loads[5].wait()
    loads[6].wait()
    for x in range(nx):
        product = weight * (ef[0, x] * en[0, x] + ef[1, x] * en[1, x] + ef[2, x] * en[2, x])
        for f in range(NF):
            dn[f, x] = dn[f, x] + cosines[f : f + 1] * product
            dn[NF + f, x] = dn[NF + f, x] + sines[f : f + 1] * product

    for i, landing in enumerate((ex_in, ey_in, ez_in)):
        pl.when(up[i][0])(e_copies[i].wait_recv)

        @pl.when(jnp.logical_not(up[i][0]))
        def _(landing=landing):
            landing[...] = jnp.zeros_like(landing)

    packed = ey_in[...]
    for x in range(nx):
        coef = hc[x]
        y0 = unpack_lane(packed, x * zt, zt, ny - 1, lane == ny - 1)
        y2 = unpack_lane(packed, (nx + x) * zt, zt, ny - 1, lane == ny - 1)
        z0 = jnp.where(sub8 == 7, ez_in[0, x : x + 1, :], 0.0)
        z1 = jnp.where(sub8 == 7, ez_in[1, x : x + 1, :], 0.0)
        rest = jnp.zeros((nz - 8, ny), jnp.float32)
        z0, z1 = jnp.concatenate([rest, z0], 0), jnp.concatenate([rest, z1], 0)
        add0, add1, add2 = y2 - z1, z0, -y0
        if x == nx - 1:
            add1 = add1 - ex_in[1]
            add2 = add2 + ex_in[0]
        hn[0, x] = hn[0, x] + coef * add0
        hn[1, x] = hn[1, x] + coef * add1
        hn[2, x] = hn[2, x] + coef * add2
    for i in range(3):
        pl.when(down[i][0])(e_copies[i].wait_send)

    for i, copy in c_copies:
        pl.when(down[i][0])(copy.wait_send)

    others = rows.at[pl.ds(0, n - 1)]
    remote(others, others, all_send, all_recv, me).wait()
    intersection = jnp.sum(rows[:, 0:1], axis=0)
    if n_gy > 1:
        grid = (n_gx, n_gy, n_gz, 1, 128)
        lower = rows[:, 1:2].reshape(grid)[:, : n_gy - 1]
        upper = rows[:, kinds - 1 : kinds].reshape(grid)[:, 1:]
        intersection = intersection + jnp.sum(lower * upper, axis=(0, 1, 2))
    port = lax.broadcasted_iota(jnp.int32, (1, 128), 1) // (128 // NP)
    owned = jnp.zeros((1, 128), jnp.float32)
    for p in range(NP):
        owned = jnp.where(port == p, (powner_ref[p] == me).astype(jnp.float32), owned)
    total = jnp.sum(owned * intersection, axis=1, keepdims=True)
    mon_out[...] = mon_ref[...] + total * phase_lanes[0:1, : 2 * NF]


def write_out(en, hn, dn, mon, en_out, hn_out, dn_out, mon_out, sems):
    parts = 4
    size = dn.shape[0] // parts
    pairs = [(dn.at[pl.ds(i * size, size)], dn_out.at[pl.ds(i * size, size)]) for i in range(parts)]
    pairs += [(en, en_out), (hn, hn_out), (mon, mon_out)]
    copies = [pltpu.make_async_copy(src, dst, sems.at[i]) for i, (src, dst) in enumerate(pairs)]
    for copy in copies:
        copy.start()
    for copy in copies:
        copy.wait()


def body(sizes, e_field, h_field, e_forward, e_coeff, h_coeff, dft_acc, design_mask,
         omega_t, port_index, port_owner, port_modes, monitor_acc):
    nx, nz, ny = e_coeff.shape
    n = sizes[0] * sizes[1] * sizes[2]
    kinds = min(sizes[1], 3)
    f32 = jnp.float32
    hbm = pl.BlockSpec(memory_space=pltpu.HBM)
    vmem = pl.BlockSpec(memory_space=pltpu.VMEM)
    far = lambda x: pltpu.with_memory_space_constraint(x, pltpu.HBM)
    held = pl.pallas_call(
        functools.partial(step, sizes),
        out_shape=[
            pltpu.VMEM(e_field.shape, f32),
            pltpu.VMEM(h_field.shape, f32),
            pltpu.VMEM(dft_acc.shape, f32),
            pltpu.VMEM(monitor_acc.shape, f32),
        ],
        in_specs=[hbm] * 12,
        out_specs=[vmem] * 4,
        scratch_shapes=[
            pltpu.VMEM(e_forward.shape, f32),
            pltpu.VMEM(e_coeff.shape, f32),
            pltpu.VMEM(h_coeff.shape, f32),
            pltpu.VMEM(port_modes.shape, f32),
            pltpu.SMEM(design_mask.shape, jnp.int32),
            pltpu.SMEM(omega_t.shape, f32),
            pltpu.SMEM(port_index.shape, jnp.int32),
            pltpu.SMEM(port_owner.shape, jnp.int32),
            pltpu.VMEM(monitor_acc.shape, f32),
            pltpu.VMEM((2, nz, ny), f32),
            pltpu.VMEM((8, 128), f32),
            pltpu.VMEM((2, nx, ny), f32),
            pltpu.VMEM((2, nz, ny), f32),
            pltpu.VMEM((8, 128), f32),
            pltpu.VMEM((2, nx, ny), f32),
            pltpu.VMEM((8, 128), f32),
            pltpu.VMEM((8, 128), f32),
            pltpu.VMEM((1, kinds, 128), f32),
            pltpu.VMEM((n, kinds, 128), f32),
            pltpu.VMEM((nz, ny), f32),
            pltpu.VMEM((nx, ny), f32),
            pltpu.VMEM((NP, ny), f32),
            pltpu.SemaphoreType.DMA((12,)),
            pltpu.SemaphoreType.DMA((3,)),
            pltpu.SemaphoreType.DMA((3,)),
            pltpu.SemaphoreType.DMA((3,)),
            pltpu.SemaphoreType.DMA((3,)),
            pltpu.SemaphoreType.DMA((3,)),
            pltpu.SemaphoreType.DMA((3,)),
            pltpu.SemaphoreType.DMA,
            pltpu.SemaphoreType.DMA,
            pltpu.SemaphoreType.REGULAR((2,)),
        ],
        compiler_params=pltpu.CompilerParams(
            collective_id=0, has_side_effects=True, vmem_limit_bytes=24 * 2**20
        ),
        name="yee_step",
    )(*map(far, (e_field, h_field, e_forward, e_coeff, h_coeff, dft_acc, port_modes,
      design_mask, omega_t, port_index, port_owner, monitor_acc)))
    shape = lambda x: jax.ShapeDtypeStruct(x.shape, f32)
    return pl.pallas_call(
        write_out,
        out_shape=[shape(x) for x in (e_field, h_field, dft_acc, monitor_acc)],
        in_specs=[vmem] * 4,
        out_specs=[hbm] * 4,
        scratch_shapes=[pltpu.SemaphoreType.DMA((7,))],
        name="write_out",
    )(*[pltpu.with_memory_space_constraint(x, pltpu.VMEM) for x in held])


def solution(mesh):
    grid = P(None, "gx", "gz", "gy")
    brick = P("gx", "gz", "gy")
    own = P(("gx", "gy", "gz"), None)
    sizes = tuple(mesh.shape[axis] for axis in ("gx", "gy", "gz"))
    in_specs = (grid, grid, grid, brick, brick, grid, brick, P(), P(), P(),
                P(None, None, "gz", "gy"), own)
    return jax.shard_map(
        functools.partial(body, sizes), mesh=mesh, in_specs=in_specs,
        out_specs=(grid, grid, grid, own), check_vma=False,
    )
```

```python
import functools

import jax
import jax.numpy as jnp
from jax import lax
from jax.experimental import pallas as pl
from jax.experimental.pallas import tpu as pltpu
from jax.sharding import PartitionSpec as P

BY = 8
NF = 8
NP = 4
UNROLL = 32


def tiles(plane):
    return [plane[8 * q : 8 * q + 8] for q in range(plane.shape[0] // 8)]


def pack_lane(fields, lane_of, lane):
    packed = jnp.zeros((8, 128), jnp.float32)
    k = 0
    for plane in fields:
        for tile in tiles(plane):
            moved = pltpu.roll(tile, (k - lane_of) % 128, 1)
            packed = jnp.where(lane == k, moved, packed)
            k += 1
    return packed


def unpack_lane(packed, first, count, lane_of, keep):
    out = [pltpu.roll(packed, (lane_of - first - q) % 128, 1) for q in range(count)]
    return jnp.where(keep, jnp.concatenate(out, 0), 0.0)


def step(
    sizes, e_hbm, h_hbm, ef_hbm, ec_hbm, hc_hbm, dft_hbm, modes_hbm,
    mask_hbm, omega_hbm, pidx_hbm, powner_hbm, mon_hbm,
    en, hn, dn, rows, aux,
    ef, ec, hc, modes, mask_ref, omega_ref, pidx_ref, powner_ref, mon_ref,
    hx_in, hy_in, hz_in, ex_in, ey_in, ez_in, hy_out, ey_out, mine,
    cx_in, cz_in, mz_in,
    load_sems, h_send, h_recv, e_send, e_recv, c_send, c_recv, all_send, all_recv,
    near_sems, far_sems, known_sems,
):
    n_gx, n_gy, n_gz = sizes
    n = n_gx * n_gy * n_gz
    kinds = rows.shape[1]
    a, b, c = lax.axis_index("gx"), lax.axis_index("gy"), lax.axis_index("gz")
    stride_x, stride_y = n_gy * n_gz, n_gz
    me = a * stride_x + b * stride_y + c
    nx, nz, ny = ec.shape
    zt = nz // 8

    lines = [(a, n_gx, stride_x), (b, n_gy, stride_y), (c, n_gz, 1)]

    def signal(sem, dev):
        pl.semaphore_signal(sem, inc=1, device_id=dev, device_id_type=pl.DeviceIdType.LOGICAL)

    def tell(line, sem):
        at, size, stride = line
        for k in range(1, size):
            signal(sem, me + (lax.rem(at + k, size) - at) * stride)

    def far_upper(axis):
        at, size, _ = lines[axis]
        if size > 2:

            @pl.when(at < size - 2)
            def _():
                pl.semaphore_wait(far_sems.at[axis], size - 2 - at)

    barrier = pltpu.get_barrier_semaphore()
    loads = [
        pltpu.make_async_copy(src, dst, load_sems.at[i])
        for i, (src, dst) in enumerate(
            [(h_hbm, hn), (e_hbm, en), (ec_hbm, ec), (modes_hbm, modes), (hc_hbm, hc), (ef_hbm, ef), (dft_hbm, dn),
             (mask_hbm, mask_ref), (omega_hbm, omega_ref), (pidx_hbm, pidx_ref), (powner_hbm, powner_ref), (mon_hbm, mon_ref)]
        )
    ]
    for at, size, stride in lines:
        for k in range(1, size):
            pl.when(at + k < size)(functools.partial(signal, barrier, me + k * stride))

    def remote(src, dst, send, recv, dev):
        return pltpu.make_async_remote_copy(
            src_ref=src, dst_ref=dst, send_sem=send, recv_sem=recv,
            device_id=dev, device_id_type=pl.DeviceIdType.LOGICAL,
        )

    up = [(a < n_gx - 1, stride_x), (b < n_gy - 1, stride_y), (c < n_gz - 1, 1)]
    down = [(a > 0, stride_x), (b > 0, stride_y), (c > 0, 1)]
    h_copies = [
        remote(src, dst, h_send.at[i], h_recv.at[i], jnp.where(up[i][0], me + up[i][1], 0))
        for i, (src, dst) in enumerate(
            [(hn.at[1:3, nx - 1], hx_in), (hy_out, hy_in), (hn.at[0:2, :, nz - 1], hz_in)]
        )
    ]
    e_copies = [
        remote(src, dst, e_send.at[i], e_recv.at[i], jnp.where(down[i][0], me - down[i][1], 0))
        for i, (src, dst) in enumerate(
            [(en.at[1:3, 0], ex_in), (ey_out, ey_in), (en.at[0:2, :, 0], ez_in)]
        )
    ]

    c_copies = [
        (i, remote(src, dst, c_send.at[k], c_recv.at[k], jnp.where(down[i][0], me - down[i][1], 0)))
        for k, (i, src, dst) in enumerate(
            [(0, ec_hbm.at[0], cx_in), (2, ec_hbm.at[:, 0], cz_in), (2, modes_hbm.at[:, 0, 0], mz_in)]
        )
    ]

    row = lax.broadcasted_iota(jnp.int32, (nz, ny), 0)
    lane = lax.broadcasted_iota(jnp.int32, (nz, ny), 1)
    lane8 = lax.broadcasted_iota(jnp.int32, (8, 128), 1)
    group = 128 // NP

    sub8 = lax.broadcasted_iota(jnp.int32, (8, 128), 0)

    @pl.when(me > 0)
    def _():
        pl.semaphore_wait(barrier, a + b + c)

    for i, copy in c_copies:
        pl.when(down[i][0])(copy.start)
    for axis, (at, size, stride) in enumerate(lines):
        for k in range(1, size if axis else 2):
            sem = (far_sems if k > 1 else near_sems).at[axis]
            pl.when(at >= k)(functools.partial(signal, sem, me - k * stride))

    for i in (0, 9, 2, 1, 3):
        loads[i].start()
    for i in (7, 8, 10, 11, 4, 5, 6):
        loads[i].start()

    loads[0].wait()
    hy_out[...] = pack_lane(
        [hn[comp, x] for comp in (0, 2) for x in range(nx)], ny - 1, lane8
    )
    for i in (2, 0, 1):

        @pl.when(up[i][0])
        def _(i=i):
            pl.semaphore_wait(near_sems.at[i], 1)
            h_copies[i].start()

    far_upper(1)
    tell(lines[1], known_sems.at[0])

    for i in (7, 8, 9, 10, 11):
        loads[i].wait()
    angle_rows = jnp.zeros((8, 128), jnp.float32)
    angle_lanes = jnp.zeros((8, 128), jnp.float32)
    for f in range(NF):
        angle_rows = jnp.where(sub8 == f, omega_ref[f], angle_rows)
        angle_lanes = jnp.where((lane8 == f) | (lane8 == f + NF), omega_ref[f], angle_lanes)
    cosines, sines = jnp.cos(angle_rows), -jnp.sin(angle_rows)
    phase_lanes = jnp.where(lane8 < NF, jnp.cos(angle_lanes), -jnp.sin(angle_lanes))
    weight = jnp.zeros((8, 128), jnp.float32)
    for k in range(ny // BY):
        weight = jnp.where(lane8 // BY == k, mask_ref[0, 0, k].astype(jnp.float32), weight)
    weight = jnp.concatenate([weight] * zt, 0)
    port = lax.broadcasted_iota(jnp.int32, (1, 128), 1) // group
    owned = jnp.zeros((1, 128), jnp.float32)
    for p in range(NP):
        owned = jnp.where(port == p, (powner_ref[p] == me).astype(jnp.float32), owned)
    aux[0:1] = owned
    aux[1:2] = phase_lanes[0:1]
    aux[2:3, : 2 * NF] = mon_ref[...]

    for i in (1, 2, 3):
        loads[i].wait()

    ports = []
    for p in range(NP):
        x_of = pidx_ref[p] - a * nx
        ports.append(((x_of >= 0) & (x_of < nx), x_of == nx, jnp.clip(x_of, 0, nx - 1)))

    def low(plane, axis):
        first = (row if axis == 0 else lane) == 0
        return plane - jnp.where(first, 0.0, pltpu.roll(plane, 1, axis))

    for x in range(nx):
        h0, h1, h2 = hn[0, x], hn[1, x], hn[2, x]
        d1 = h1 - hn[1, x - 1] if x else h1
        d2 = h2 - hn[2, x - 1] if x else h2
        coef = ec[x]
        en[0, x] = en[0, x] - coef * (low(h2, 1) - low(h1, 0))
        en[1, x] = en[1, x] - coef * (low(h0, 0) - d2)
        en[2, x] = en[2, x] - coef * (d1 - low(h0, 1))

    partial = []
    for p, (inside, _, at) in enumerate(ports):
        both = modes[p, 0] * en[1, at] + modes[p, 1] * en[2, at]
        partial.append(jnp.where(inside, functools.reduce(jnp.add, tiles(both)), 0.0))

    def column(planes, lane_of):
        packed = jnp.zeros((8, 128), jnp.float32)
        for p, plane in enumerate(planes):
            for q, tile in enumerate(tiles(plane)):
                to = p * group + q
                packed = jnp.where(lane8 == to, pltpu.roll(tile, (to - lane_of) % 128, 1), packed)
        packed = pltpu.roll(packed, 0, 1, stride=zt, stride_axis=0)
        return jnp.sum(packed, axis=0, keepdims=True)

    columns = []
    if n_gy > 1:
        below = [jnp.where(inside, -hn[0, at], 0.0) for inside, _, at in ports]
        above = [modes[p, 1] * ec[at] for p, (_, _, at) in enumerate(ports)]
        if n_gy == 2:
            edge = jnp.broadcast_to(b == 0, (nz, ny))
            both = [jnp.where(edge, pltpu.roll(u, 1, 1), v) for u, v in zip(below, above)]
            columns = [column(both, 0)]
        else:
            columns = [column(below, ny - 1), column(above, 0)]

    x_parts = [
        jnp.where(over, modes[p, 1] * hn[1, nx - 1] - modes[p, 0] * hn[2, nx - 1], 0.0)
        for p, (_, over, _) in enumerate(ports)
    ]
    z_parts = [jnp.where(inside, hn[0, at, nz - 1 : nz], 0.0) for inside, _, at in ports]

    if n_gy > 1:
        pl.semaphore_wait(known_sems.at[0], n_gy - 1)
    far_upper(2)
    tell(lines[2], known_sems.at[1])

    for (i, copy), landing in zip(c_copies, (cx_in, cz_in, mz_in)):
        pl.when(up[i][0])(copy.wait_recv)

        @pl.when(jnp.logical_not(up[i][0]))
        def _(landing=landing):
            landing[...] = jnp.zeros_like(landing)

    share = jnp.zeros((8, 128), jnp.float32)
    for p, (_, _, at) in enumerate(ports):
        x_part = functools.reduce(jnp.add, tiles(cx_in[...] * x_parts[p]))
        z_part = mz_in[p : p + 1] * cz_in[pl.ds(at, 1)] * z_parts[p]
        total = partial[p] + x_part + jnp.where(sub8 == 0, z_part, 0.0)
        width = 128
        while width > group:
            width //= 2
            total = total + pltpu.roll(total, width, 1)
        share = jnp.where(lane8 // group == p, total, share)
    mine[0, 0:1] = jnp.sum(share, axis=0, keepdims=True)
    for k, vector in enumerate(columns):
        mine[0, k + 1 : k + 2] = vector
    rows[pl.ds(me, 1)] = mine[...]

    if n_gz > 1:
        pl.semaphore_wait(known_sems.at[1], n_gz - 1)

    for k in range(1, n_gx):
        pl.when(a >= k)(functools.partial(signal, known_sems.at[2], me - k * stride_x))

    def send_rows(plane):
        def send_row(k, _):
            to = plane * stride_x + k
            pl.when(to != me)(remote(mine.at[0], rows.at[me], all_send, all_recv, to).start)
            return 0

        lax.fori_loop(0, stride_x, send_row, 0, unroll=n <= UNROLL)

    for plane in range(n_gx):
        pl.when(plane <= a)(functools.partial(send_rows, plane))

    for i, landing in enumerate((hx_in, hy_in, hz_in)):
        pl.when(down[i][0])(h_copies[i].wait_recv)

        @pl.when(jnp.logical_not(down[i][0]))
        def _(landing=landing):
            landing[...] = jnp.zeros_like(landing)

    packed = hy_in[...]
    for x in range(nx):
        coef = ec[x]
        y0 = unpack_lane(packed, x * zt, zt, 0, lane == 0)
        y2 = unpack_lane(packed, (nx + x) * zt, zt, 0, lane == 0)
        z0 = jnp.where(sub8 == 0, hz_in[0, x : x + 1, :], 0.0)
        z1 = jnp.where(sub8 == 0, hz_in[1, x : x + 1, :], 0.0)
        rest = jnp.zeros((nz - 8, ny), jnp.float32)
        z0, z1 = jnp.concatenate([z0, rest], 0), jnp.concatenate([z1, rest], 0)
        add0, add1, add2 = y2 - z1, z0, -y0
        if x == 0:
            add1 = add1 - hx_in[1]
            add2 = add2 + hx_in[0]
        en[0, x] = en[0, x] + coef * add0
        en[1, x] = en[1, x] + coef * add1
        en[2, x] = en[2, x] + coef * add2
        if x == 0:
            pl.when(down[0][0])(e_copies[0].start)

    pl.when(down[2][0])(e_copies[2].start)
    ey_out[...] = pack_lane([en[comp, x] for comp in (0, 2) for x in range(nx)], 0, lane8)
    pl.when(down[1][0])(e_copies[1].start)

    for i in range(3):
        pl.when(up[i][0])(h_copies[i].wait_send)
    loads[4].wait()

    def high(plane, axis):
        last = (row == nz - 1) if axis == 0 else (lane == ny - 1)
        return jnp.where(last, 0.0, pltpu.roll(plane, plane.shape[axis] - 1, axis)) - plane

    for x in range(nx):
        e0, e1, e2 = en[0, x], en[1, x], en[2, x]
        d1 = en[1, x + 1] - e1 if x < nx - 1 else -e1
        d2 = en[2, x + 1] - e2 if x < nx - 1 else -e2
        coef = hc[x]
        hn[0, x] = hn[0, x] + coef * (high(e2, 1) - high(e1, 0))
        hn[1, x] = hn[1, x] + coef * (high(e0, 0) - d2)
        hn[2, x] = hn[2, x] + coef * (d1 - high(e0, 1))

    loads[5].wait()
    loads[6].wait()
    for x in range(nx):
        product = weight * (ef[0, x] * en[0, x] + ef[1, x] * en[1, x] + ef[2, x] * en[2, x])
        for f in range(NF):
            dn[f, x] = dn[f, x] + cosines[f : f + 1] * product
            dn[NF + f, x] = dn[NF + f, x] + sines[f : f + 1] * product

    @pl.when(a < n_gx - 1)
    def _():
        pl.semaphore_wait(known_sems.at[2], n_gx - 1 - a)

    for plane in range(1, n_gx):
        pl.when(plane > a)(functools.partial(send_rows, plane))

    for i, landing in enumerate((ex_in, ey_in, ez_in)):
        pl.when(up[i][0])(e_copies[i].wait_recv)

        @pl.when(jnp.logical_not(up[i][0]))
        def _(landing=landing):
            landing[...] = jnp.zeros_like(landing)

    packed = ey_in[...]
    for x in range(nx):
        coef = hc[x]
        y0 = unpack_lane(packed, x * zt, zt, ny - 1, lane == ny - 1)
        y2 = unpack_lane(packed, (nx + x) * zt, zt, ny - 1, lane == ny - 1)
        z0 = jnp.where(sub8 == 7, ez_in[0, x : x + 1, :], 0.0)
        z1 = jnp.where(sub8 == 7, ez_in[1, x : x + 1, :], 0.0)
        rest = jnp.zeros((nz - 8, ny), jnp.float32)
        z0, z1 = jnp.concatenate([rest, z0], 0), jnp.concatenate([rest, z1], 0)
        add0, add1, add2 = y2 - z1, z0, -y0
        if x == nx - 1:
            add1 = add1 - ex_in[1]
            add2 = add2 + ex_in[0]
        hn[0, x] = hn[0, x] + coef * add0
        hn[1, x] = hn[1, x] + coef * add1
        hn[2, x] = hn[2, x] + coef * add2
    for i in range(3):
        pl.when(down[i][0])(e_copies[i].wait_send)

    for i, copy in c_copies:
        pl.when(down[i][0])(copy.wait_send)

    others = rows.at[pl.ds(0, n - 1)]
    remote(others, others, all_send, all_recv, me).wait()


def write_out(sizes, en, hn, dn, rows, aux, en_out, hn_out, dn_out, mon_out, mon, sems):
    parts = 4
    size = dn.shape[0] // parts
    pairs = [(dn.at[pl.ds(i * size, size)], dn_out.at[pl.ds(i * size, size)]) for i in range(parts)]
    pairs += [(en, en_out), (hn, hn_out), (mon, mon_out)]
    copies = [pltpu.make_async_copy(src, dst, sems.at[i]) for i, (src, dst) in enumerate(pairs)]
    for copy in copies[:-1]:
        copy.start()
    kinds = rows.shape[1]
    n_gy = sizes[1]
    intersection = jnp.sum(rows[:, 0:1], axis=0)
    if n_gy > 1:
        grid = (*sizes, 1, 128)
        lower = rows[:, 1:2].reshape(grid)[:, : n_gy - 1]
        upper = rows[:, kinds - 1 : kinds].reshape(grid)[:, 1:]
        intersection = intersection + jnp.sum(lower * upper, axis=(0, 1, 2))
    total = jnp.sum(aux[0:1] * intersection, axis=1, keepdims=True)
    mon[...] = aux[2:3, : 2 * NF] + total * aux[1:2, : 2 * NF]
    copies[-1].start()
    for copy in copies:
        copy.wait()


def body(sizes, e_field, h_field, e_forward, e_coeff, h_coeff, dft_acc, design_mask,
         omega_t, port_index, port_owner, port_modes, monitor_acc):
    nx, nz, ny = e_coeff.shape
    n = sizes[0] * sizes[1] * sizes[2]
    kinds = min(sizes[1], 3)
    f32 = jnp.float32
    hbm = pl.BlockSpec(memory_space=pltpu.HBM)
    vmem = pl.BlockSpec(memory_space=pltpu.VMEM)
    far = lambda x: pltpu.with_memory_space_constraint(x, pltpu.HBM)
    held = pl.pallas_call(
        functools.partial(step, sizes),
        out_shape=[
            pltpu.VMEM(e_field.shape, f32),
            pltpu.VMEM(h_field.shape, f32),
            pltpu.VMEM(dft_acc.shape, f32),
            pltpu.VMEM((n, kinds, 128), f32),
            pltpu.VMEM((3, 128), f32),
        ],
        in_specs=[hbm] * 12,
        out_specs=[vmem] * 5,
        scratch_shapes=[
            pltpu.VMEM(e_forward.shape, f32),
            pltpu.VMEM(e_coeff.shape, f32),
            pltpu.VMEM(h_coeff.shape, f32),
            pltpu.VMEM(port_modes.shape, f32),
            pltpu.SMEM(design_mask.shape, jnp.int32),
            pltpu.SMEM(omega_t.shape, f32),
            pltpu.SMEM(port_index.shape, jnp.int32),
            pltpu.SMEM(port_owner.shape, jnp.int32),
            pltpu.VMEM(monitor_acc.shape, f32),
            pltpu.VMEM((2, nz, ny), f32),
            pltpu.VMEM((8, 128), f32),
            pltpu.VMEM((2, nx, ny), f32),
            pltpu.VMEM((2, nz, ny), f32),
            pltpu.VMEM((8, 128), f32),
            pltpu.VMEM((2, nx, ny), f32),
            pltpu.VMEM((8, 128), f32),
            pltpu.VMEM((8, 128), f32),
            pltpu.VMEM((1, kinds, 128), f32),
            pltpu.VMEM((nz, ny), f32),
            pltpu.VMEM((nx, ny), f32),
            pltpu.VMEM((NP, ny), f32),
            pltpu.SemaphoreType.DMA((12,)),
            pltpu.SemaphoreType.DMA((3,)),
            pltpu.SemaphoreType.DMA((3,)),
            pltpu.SemaphoreType.DMA((3,)),
            pltpu.SemaphoreType.DMA((3,)),
            pltpu.SemaphoreType.DMA((3,)),
            pltpu.SemaphoreType.DMA((3,)),
            pltpu.SemaphoreType.DMA,
            pltpu.SemaphoreType.DMA,
            pltpu.SemaphoreType.REGULAR((3,)),
            pltpu.SemaphoreType.REGULAR((3,)),
            pltpu.SemaphoreType.REGULAR((3,)),
        ],
        compiler_params=pltpu.CompilerParams(
            collective_id=0, has_side_effects=True, vmem_limit_bytes=24 * 2**20
        ),
        name="yee_step",
    )(*map(far, (e_field, h_field, e_forward, e_coeff, h_coeff, dft_acc, port_modes,
      design_mask, omega_t, port_index, port_owner, monitor_acc)))
    shape = lambda x: jax.ShapeDtypeStruct(x.shape, f32)
    return pl.pallas_call(
        functools.partial(write_out, sizes),
        out_shape=[shape(x) for x in (e_field, h_field, dft_acc, monitor_acc)],
        in_specs=[vmem] * 5,
        out_specs=[hbm] * 4,
        scratch_shapes=[pltpu.VMEM(monitor_acc.shape, f32), pltpu.SemaphoreType.DMA((7,))],
        name="write_out",
    )(*[pltpu.with_memory_space_constraint(x, pltpu.VMEM) for x in held])


def solution(mesh):
    grid = P(None, "gx", "gz", "gy")
    brick = P("gx", "gz", "gy")
    own = P(("gx", "gy", "gz"), None)
    sizes = tuple(mesh.shape[axis] for axis in ("gx", "gy", "gz"))
    in_specs = (grid, grid, grid, brick, brick, grid, brick, P(), P(), P(),
                P(None, None, "gz", "gy"), own)
    return jax.shard_map(
        functools.partial(body, sizes), mesh=mesh, in_specs=in_specs,
        out_specs=(grid, grid, grid, own), check_vma=False,
    )
```

```python
import functools

import jax
import jax.numpy as jnp
from jax import lax
from jax.experimental import pallas as pl
from jax.experimental.pallas import tpu as pltpu
from jax.sharding import PartitionSpec as P

BY = 8
NF = 8
NP = 4
UNROLL = 32


def tiles(plane):
    return [plane[8 * q : 8 * q + 8] for q in range(plane.shape[0] // 8)]


def pack_lane(fields, lane_of, lane):
    packed = jnp.zeros((8, 128), jnp.float32)
    k = 0
    for plane in fields:
        for tile in tiles(plane):
            moved = pltpu.roll(tile, (k - lane_of) % 128, 1)
            packed = jnp.where(lane == k, moved, packed)
            k += 1
    return packed


def unpack_lane(packed, first, count, lane_of, keep):
    out = [pltpu.roll(packed, (lane_of - first - q) % 128, 1) for q in range(count)]
    return jnp.where(keep, jnp.concatenate(out, 0), 0.0)


def step(
    sizes, e_hbm, h_hbm, ef_hbm, ec_hbm, hc_hbm, dft_hbm, modes_hbm,
    mask_hbm, omega_hbm, pidx_hbm, powner_hbm, mon_hbm,
    en, hn, dn, rows, aux,
    ef, ec, hc, modes, mask_ref, omega_ref, pidx_ref, powner_ref, mon_ref,
    hx_in, hy_in, hz_in, ex_in, ey_in, ez_in, hy_out, ey_out, mine,
    cx_in, cz_in, mz_in, cx_out,
    load_sems, h_send, h_recv, e_send, e_recv, c_send, c_recv, all_send, all_recv,
    near_sems, far_sems, known_sems,
):
    n_gx, n_gy, n_gz = sizes
    n = n_gx * n_gy * n_gz
    kinds = rows.shape[1]
    a, b, c = lax.axis_index("gx"), lax.axis_index("gy"), lax.axis_index("gz")
    stride_x, stride_y = n_gy * n_gz, n_gz
    me = a * stride_x + b * stride_y + c
    nx, nz, ny = ec.shape
    zt = nz // 8

    lines = [(a, n_gx, stride_x), (b, n_gy, stride_y), (c, n_gz, 1)]

    def signal(sem, dev):
        pl.semaphore_signal(sem, inc=1, device_id=dev, device_id_type=pl.DeviceIdType.LOGICAL)

    def tell(line, sem):
        at, size, stride = line
        for k in range(1, size):
            signal(sem, me + (lax.rem(at + k, size) - at) * stride)

    def tell_line():
        for k in range(1, n_gz):
            pl.when(c + k < n_gz)(functools.partial(signal, known_sems.at[1], me + k))
            pl.when(c >= k)(functools.partial(signal, known_sems.at[3], me - k))

    def far_upper(axis):
        at, size, _ = lines[axis]
        if size > 2:

            @pl.when(at < size - 2)
            def _():
                pl.semaphore_wait(far_sems.at[axis], size - 2 - at)

    barrier = pltpu.get_barrier_semaphore()
    loads = [
        pltpu.make_async_copy(src, dst, load_sems.at[i])
        for i, (src, dst) in enumerate(
            [(h_hbm, hn), (e_hbm, en), (ec_hbm, ec), (modes_hbm, modes), (hc_hbm, hc), (ef_hbm, ef), (dft_hbm, dn),
             (mask_hbm, mask_ref), (omega_hbm, omega_ref), (pidx_hbm, pidx_ref), (powner_hbm, powner_ref), (mon_hbm, mon_ref)]
        )
    ]
    first = pltpu.make_async_copy(ec_hbm.at[0], cx_out, load_sems.at[12])
    first.start()
    for at, size, stride in lines:
        for k in range(1, size):
            pl.when(at + k < size)(functools.partial(signal, barrier, me + k * stride))

    def remote(src, dst, send, recv, dev):
        return pltpu.make_async_remote_copy(
            src_ref=src, dst_ref=dst, send_sem=send, recv_sem=recv,
            device_id=dev, device_id_type=pl.DeviceIdType.LOGICAL,
        )

    up = [(a < n_gx - 1, stride_x), (b < n_gy - 1, stride_y), (c < n_gz - 1, 1)]
    down = [(a > 0, stride_x), (b > 0, stride_y), (c > 0, 1)]
    h_copies = [
        remote(src, dst, h_send.at[i], h_recv.at[i], jnp.where(up[i][0], me + up[i][1], 0))
        for i, (src, dst) in enumerate(
            [(hn.at[1:3, nx - 1], hx_in), (hy_out, hy_in), (hn.at[0:2, :, nz - 1], hz_in)]
        )
    ]
    e_copies = [
        remote(src, dst, e_send.at[i], e_recv.at[i], jnp.where(down[i][0], me - down[i][1], 0))
        for i, (src, dst) in enumerate(
            [(en.at[1:3, 0], ex_in), (ey_out, ey_in), (en.at[0:2, :, 0], ez_in)]
        )
    ]

    c_copies = [
        (i, remote(src, dst, c_send.at[k], c_recv.at[k], jnp.where(down[i][0], me - down[i][1], 0)))
        for k, (i, src, dst) in enumerate(
            [(0, cx_out, cx_in), (2, ec_hbm.at[:, 0], cz_in), (2, modes_hbm.at[:, 0, 0], mz_in)]
        )
    ]

    row = lax.broadcasted_iota(jnp.int32, (nz, ny), 0)
    lane = lax.broadcasted_iota(jnp.int32, (nz, ny), 1)
    lane8 = lax.broadcasted_iota(jnp.int32, (8, 128), 1)
    group = 128 // NP

    sub8 = lax.broadcasted_iota(jnp.int32, (8, 128), 0)

    @pl.when(me > 0)
    def _():
        pl.semaphore_wait(barrier, a + b + c)

    for i, copy in c_copies[1:]:
        pl.when(down[i][0])(copy.start)
    for axis, (at, size, stride) in enumerate(lines):
        for k in range(1, size if axis else 2):
            sem = (far_sems if k > 1 else near_sems).at[axis]
            pl.when(at >= k)(functools.partial(signal, sem, me - k * stride))
    first.wait()
    pl.when(down[0][0])(c_copies[0][1].start)

    for i in (0, 9, 2, 1, 3):
        loads[i].start()
    for i in (7, 8, 10, 11, 4, 5, 6):
        loads[i].start()

    loads[0].wait()
    hy_out[...] = pack_lane(
        [hn[comp, x] for comp in (0, 2) for x in range(nx)], ny - 1, lane8
    )
    for i in (2, 0, 1):

        @pl.when(up[i][0])
        def _(i=i):
            pl.semaphore_wait(near_sems.at[i], 1)
            h_copies[i].start()

    far_upper(1)
    tell(lines[1], known_sems.at[0])

    for i in (7, 8, 9, 10, 11):
        loads[i].wait()
    angle_rows = jnp.zeros((8, 128), jnp.float32)
    angle_lanes = jnp.zeros((8, 128), jnp.float32)
    for f in range(NF):
        angle_rows = jnp.where(sub8 == f, omega_ref[f], angle_rows)
        angle_lanes = jnp.where((lane8 == f) | (lane8 == f + NF), omega_ref[f], angle_lanes)
    cosines, sines = jnp.cos(angle_rows), -jnp.sin(angle_rows)
    phase_lanes = jnp.where(lane8 < NF, jnp.cos(angle_lanes), -jnp.sin(angle_lanes))
    weight = jnp.zeros((8, 128), jnp.float32)
    for k in range(ny // BY):
        weight = jnp.where(lane8 // BY == k, mask_ref[0, 0, k].astype(jnp.float32), weight)
    weight = jnp.concatenate([weight] * zt, 0)
    port = lax.broadcasted_iota(jnp.int32, (1, 128), 1) // group
    owned = jnp.zeros((1, 128), jnp.float32)
    for p in range(NP):
        owned = jnp.where(port == p, (powner_ref[p] == me).astype(jnp.float32), owned)
    aux[0:1] = owned
    aux[1:2] = phase_lanes[0:1]
    aux[2:3, : 2 * NF] = mon_ref[...]

    for i in (1, 2, 3):
        loads[i].wait()

    ports = []
    for p in range(NP):
        x_of = pidx_ref[p] - a * nx
        ports.append(((x_of >= 0) & (x_of < nx), x_of == nx, jnp.clip(x_of, 0, nx - 1)))

    def low(plane, axis):
        first = (row if axis == 0 else lane) == 0
        return plane - jnp.where(first, 0.0, pltpu.roll(plane, 1, axis))

    for x in range(nx):
        h0, h1, h2 = hn[0, x], hn[1, x], hn[2, x]
        d1 = h1 - hn[1, x - 1] if x else h1
        d2 = h2 - hn[2, x - 1] if x else h2
        coef = ec[x]
        en[0, x] = en[0, x] - coef * (low(h2, 1) - low(h1, 0))
        en[1, x] = en[1, x] - coef * (low(h0, 0) - d2)
        en[2, x] = en[2, x] - coef * (d1 - low(h0, 1))

    partial = []
    for p, (inside, _, at) in enumerate(ports):
        both = modes[p, 0] * en[1, at] + modes[p, 1] * en[2, at]
        partial.append(jnp.where(inside, functools.reduce(jnp.add, tiles(both)), 0.0))

    def column(planes, lane_of):
        packed = jnp.zeros((8, 128), jnp.float32)
        for p, plane in enumerate(planes):
            for q, tile in enumerate(tiles(plane)):
                to = p * group + q
                packed = jnp.where(lane8 == to, pltpu.roll(tile, (to - lane_of) % 128, 1), packed)
        packed = pltpu.roll(packed, 0, 1, stride=zt, stride_axis=0)
        return jnp.sum(packed, axis=0, keepdims=True)

    columns = []
    if n_gy > 1:
        below = [jnp.where(inside, -hn[0, at], 0.0) for inside, _, at in ports]
        above = [modes[p, 1] * ec[at] for p, (_, _, at) in enumerate(ports)]
        if n_gy == 2:
            edge = jnp.broadcast_to(b == 0, (nz, ny))
            both = [jnp.where(edge, pltpu.roll(u, 1, 1), v) for u, v in zip(below, above)]
            columns = [column(both, 0)]
        else:
            columns = [column(below, ny - 1), column(above, 0)]

    x_parts = [
        jnp.where(over, modes[p, 1] * hn[1, nx - 1] - modes[p, 0] * hn[2, nx - 1], 0.0)
        for p, (_, over, _) in enumerate(ports)
    ]
    z_parts = [jnp.where(inside, hn[0, at, nz - 1 : nz], 0.0) for inside, _, at in ports]

    if n_gy > 1:
        pl.semaphore_wait(known_sems.at[0], n_gy - 1)
    far_upper(2)
    tell_line()

    for (i, copy), landing in zip(c_copies, (cx_in, cz_in, mz_in)):
        pl.when(up[i][0])(copy.wait_recv)

        @pl.when(jnp.logical_not(up[i][0]))
        def _(landing=landing):
            landing[...] = jnp.zeros_like(landing)

    share = jnp.zeros((8, 128), jnp.float32)
    for p, (_, _, at) in enumerate(ports):
        x_part = functools.reduce(jnp.add, tiles(cx_in[...] * x_parts[p]))
        z_part = mz_in[p : p + 1] * cz_in[pl.ds(at, 1)] * z_parts[p]
        total = partial[p] + x_part + jnp.where(sub8 == 0, z_part, 0.0)
        width = 128
        while width > group:
            width //= 2
            total = total + pltpu.roll(total, width, 1)
        share = jnp.where(lane8 // group == p, total, share)
    mine[0, 0:1] = jnp.sum(share, axis=0, keepdims=True)
    for k, vector in enumerate(columns):
        mine[0, k + 1 : k + 2] = vector
    rows[pl.ds(me, 1)] = mine[...]

    @pl.when(c > 0)
    def _():
        pl.semaphore_wait(known_sems.at[1], c)

    def send_rows(plane, part):
        def send_row(k, _):
            to = plane * stride_x + k
            near = k % n_gz <= c
            wanted = {"near": near, "far": jnp.logical_not(near), "all": True}[part]
            pl.when((to != me) & wanted)(remote(mine.at[0], rows.at[me], all_send, all_recv, to).start)
            return 0

        lax.fori_loop(0, stride_x, send_row, 0, unroll=n <= UNROLL)

    for plane in range(n_gx):
        pl.when(plane <= a)(functools.partial(send_rows, plane, "near"))

    @pl.when(c < n_gz - 1)
    def _():
        pl.semaphore_wait(known_sems.at[3], n_gz - 1 - c)

    for plane in range(n_gx):
        pl.when(plane <= a)(functools.partial(send_rows, plane, "far"))

    for k in range(1, n_gx):
        pl.when(a >= k)(functools.partial(signal, known_sems.at[2], me - k * stride_x))

    for i, landing in enumerate((hx_in, hy_in, hz_in)):
        pl.when(down[i][0])(h_copies[i].wait_recv)

        @pl.when(jnp.logical_not(down[i][0]))
        def _(landing=landing):
            landing[...] = jnp.zeros_like(landing)

    packed = hy_in[...]
    for x in range(nx):
        coef = ec[x]
        y0 = unpack_lane(packed, x * zt, zt, 0, lane == 0)
        y2 = unpack_lane(packed, (nx + x) * zt, zt, 0, lane == 0)
        z0 = jnp.where(sub8 == 0, hz_in[0, x : x + 1, :], 0.0)
        z1 = jnp.where(sub8 == 0, hz_in[1, x : x + 1, :], 0.0)
        rest = jnp.zeros((nz - 8, ny), jnp.float32)
        z0, z1 = jnp.concatenate([z0, rest], 0), jnp.concatenate([z1, rest], 0)
        add0, add1, add2 = y2 - z1, z0, -y0
        if x == 0:
            add1 = add1 - hx_in[1]
            add2 = add2 + hx_in[0]
        en[0, x] = en[0, x] + coef * add0
        en[1, x] = en[1, x] + coef * add1
        en[2, x] = en[2, x] + coef * add2
        if x == 0:
            pl.when(down[0][0])(e_copies[0].start)

    pl.when(down[2][0])(e_copies[2].start)
    ey_out[...] = pack_lane([en[comp, x] for comp in (0, 2) for x in range(nx)], 0, lane8)
    pl.when(down[1][0])(e_copies[1].start)

    for i in range(3):
        pl.when(up[i][0])(h_copies[i].wait_send)
    loads[4].wait()

    def high(plane, axis):
        last = (row == nz - 1) if axis == 0 else (lane == ny - 1)
        return jnp.where(last, 0.0, pltpu.roll(plane, plane.shape[axis] - 1, axis)) - plane

    for x in range(nx):
        e0, e1, e2 = en[0, x], en[1, x], en[2, x]
        d1 = en[1, x + 1] - e1 if x < nx - 1 else -e1
        d2 = en[2, x + 1] - e2 if x < nx - 1 else -e2
        coef = hc[x]
        hn[0, x] = hn[0, x] + coef * (high(e2, 1) - high(e1, 0))
        hn[1, x] = hn[1, x] + coef * (high(e0, 0) - d2)
        hn[2, x] = hn[2, x] + coef * (d1 - high(e0, 1))

    loads[5].wait()
    loads[6].wait()
    for x in range(nx):
        product = weight * (ef[0, x] * en[0, x] + ef[1, x] * en[1, x] + ef[2, x] * en[2, x])
        for f in range(NF):
            dn[f, x] = dn[f, x] + cosines[f : f + 1] * product
            dn[NF + f, x] = dn[NF + f, x] + sines[f : f + 1] * product

    @pl.when(a < n_gx - 1)
    def _():
        pl.semaphore_wait(known_sems.at[2], n_gx - 1 - a)

    for plane in range(1, n_gx):
        pl.when(plane > a)(functools.partial(send_rows, plane, "all"))

    for i, landing in enumerate((ex_in, ey_in, ez_in)):
        pl.when(up[i][0])(e_copies[i].wait_recv)

        @pl.when(jnp.logical_not(up[i][0]))
        def _(landing=landing):
            landing[...] = jnp.zeros_like(landing)

    packed = ey_in[...]
    for x in range(nx):
        coef = hc[x]
        y0 = unpack_lane(packed, x * zt, zt, ny - 1, lane == ny - 1)
        y2 = unpack_lane(packed, (nx + x) * zt, zt, ny - 1, lane == ny - 1)
        z0 = jnp.where(sub8 == 7, ez_in[0, x : x + 1, :], 0.0)
        z1 = jnp.where(sub8 == 7, ez_in[1, x : x + 1, :], 0.0)
        rest = jnp.zeros((nz - 8, ny), jnp.float32)
        z0, z1 = jnp.concatenate([rest, z0], 0), jnp.concatenate([rest, z1], 0)
        add0, add1, add2 = y2 - z1, z0, -y0
        if x == nx - 1:
            add1 = add1 - ex_in[1]
            add2 = add2 + ex_in[0]
        hn[0, x] = hn[0, x] + coef * add0
        hn[1, x] = hn[1, x] + coef * add1
        hn[2, x] = hn[2, x] + coef * add2
    for i in range(3):
        pl.when(down[i][0])(e_copies[i].wait_send)

    for i, copy in c_copies:
        pl.when(down[i][0])(copy.wait_send)

    others = rows.at[pl.ds(0, n - 1)]
    remote(others, others, all_send, all_recv, me).wait()


def write_out(sizes, en, hn, dn, rows, aux, en_out, hn_out, dn_out, mon_out, mon, sems):
    parts = 4
    size = dn.shape[0] // parts
    pairs = [(dn.at[pl.ds(i * size, size)], dn_out.at[pl.ds(i * size, size)]) for i in range(parts)]
    pairs += [(en, en_out), (hn, hn_out), (mon, mon_out)]
    copies = [pltpu.make_async_copy(src, dst, sems.at[i]) for i, (src, dst) in enumerate(pairs)]
    for copy in copies[:-1]:
        copy.start()
    kinds = rows.shape[1]
    n_gy = sizes[1]
    intersection = jnp.sum(rows[:, 0:1], axis=0)
    if n_gy > 1:
        grid = (*sizes, 1, 128)
        lower = rows[:, 1:2].reshape(grid)[:, : n_gy - 1]
        upper = rows[:, kinds - 1 : kinds].reshape(grid)[:, 1:]
        intersection = intersection + jnp.sum(lower * upper, axis=(0, 1, 2))
    total = jnp.sum(aux[0:1] * intersection, axis=1, keepdims=True)
    mon[...] = aux[2:3, : 2 * NF] + total * aux[1:2, : 2 * NF]
    copies[-1].start()
    for copy in copies:
        copy.wait()


def body(sizes, e_field, h_field, e_forward, e_coeff, h_coeff, dft_acc, design_mask,
         omega_t, port_index, port_owner, port_modes, monitor_acc):
    nx, nz, ny = e_coeff.shape
    n = sizes[0] * sizes[1] * sizes[2]
    kinds = min(sizes[1], 3)
    f32 = jnp.float32
    hbm = pl.BlockSpec(memory_space=pltpu.HBM)
    vmem = pl.BlockSpec(memory_space=pltpu.VMEM)
    far = lambda x: pltpu.with_memory_space_constraint(x, pltpu.HBM)
    held = pl.pallas_call(
        functools.partial(step, sizes),
        out_shape=[
            pltpu.VMEM(e_field.shape, f32),
            pltpu.VMEM(h_field.shape, f32),
            pltpu.VMEM(dft_acc.shape, f32),
            pltpu.VMEM((n, kinds, 128), f32),
            pltpu.VMEM((3, 128), f32),
        ],
        in_specs=[hbm] * 12,
        out_specs=[vmem] * 5,
        scratch_shapes=[
            pltpu.VMEM(e_forward.shape, f32),
            pltpu.VMEM(e_coeff.shape, f32),
            pltpu.VMEM(h_coeff.shape, f32),
            pltpu.VMEM(port_modes.shape, f32),
            pltpu.SMEM(design_mask.shape, jnp.int32),
            pltpu.SMEM(omega_t.shape, f32),
            pltpu.SMEM(port_index.shape, jnp.int32),
            pltpu.SMEM(port_owner.shape, jnp.int32),
            pltpu.VMEM(monitor_acc.shape, f32),
            pltpu.VMEM((2, nz, ny), f32),
            pltpu.VMEM((8, 128), f32),
            pltpu.VMEM((2, nx, ny), f32),
            pltpu.VMEM((2, nz, ny), f32),
            pltpu.VMEM((8, 128), f32),
            pltpu.VMEM((2, nx, ny), f32),
            pltpu.VMEM((8, 128), f32),
            pltpu.VMEM((8, 128), f32),
            pltpu.VMEM((1, kinds, 128), f32),
            pltpu.VMEM((nz, ny), f32),
            pltpu.VMEM((nx, ny), f32),
            pltpu.VMEM((NP, ny), f32),
            pltpu.VMEM((nz, ny), f32),
            pltpu.SemaphoreType.DMA((13,)),
            pltpu.SemaphoreType.DMA((3,)),
            pltpu.SemaphoreType.DMA((3,)),
            pltpu.SemaphoreType.DMA((3,)),
            pltpu.SemaphoreType.DMA((3,)),
            pltpu.SemaphoreType.DMA((3,)),
            pltpu.SemaphoreType.DMA((3,)),
            pltpu.SemaphoreType.DMA,
            pltpu.SemaphoreType.DMA,
            pltpu.SemaphoreType.REGULAR((3,)),
            pltpu.SemaphoreType.REGULAR((3,)),
            pltpu.SemaphoreType.REGULAR((4,)),
        ],
        compiler_params=pltpu.CompilerParams(
            collective_id=0, has_side_effects=True, vmem_limit_bytes=24 * 2**20
        ),
        name="yee_step",
    )(*map(far, (e_field, h_field, e_forward, e_coeff, h_coeff, dft_acc, port_modes,
      design_mask, omega_t, port_index, port_owner, monitor_acc)))
    shape = lambda x: jax.ShapeDtypeStruct(x.shape, f32)
    return pl.pallas_call(
        functools.partial(write_out, sizes),
        out_shape=[shape(x) for x in (e_field, h_field, dft_acc, monitor_acc)],
        in_specs=[vmem] * 5,
        out_specs=[hbm] * 4,
        scratch_shapes=[pltpu.VMEM(monitor_acc.shape, f32), pltpu.SemaphoreType.DMA((7,))],
        name="write_out",
    )(*[pltpu.with_memory_space_constraint(x, pltpu.VMEM) for x in held])


def solution(mesh):
    grid = P(None, "gx", "gz", "gy")
    brick = P("gx", "gz", "gy")
    own = P(("gx", "gy", "gz"), None)
    sizes = tuple(mesh.shape[axis] for axis in ("gx", "gy", "gz"))
    in_specs = (grid, grid, grid, brick, brick, grid, brick, P(), P(), P(),
                P(None, None, "gz", "gy"), own)
    return jax.shard_map(
        functools.partial(body, sizes), mesh=mesh, in_specs=in_specs,
        out_specs=(grid, grid, grid, own), check_vma=False,
    )
```

```python
import functools

import jax
import jax.numpy as jnp
from jax import lax
from jax.experimental import pallas as pl
from jax.experimental.pallas import tpu as pltpu
from jax.sharding import PartitionSpec as P

BY = 8
NF = 8
NP = 4
UNROLL = 32


def tiles(plane):
    return [plane[8 * q : 8 * q + 8] for q in range(plane.shape[0] // 8)]


def pack_lane(fields, lane_of, lane):
    packed = jnp.zeros((8, 128), jnp.float32)
    k = 0
    for plane in fields:
        for tile in tiles(plane):
            moved = pltpu.roll(tile, (k - lane_of) % 128, 1)
            packed = jnp.where(lane == k, moved, packed)
            k += 1
    return packed


def unpack_lane(packed, first, count, lane_of, keep):
    out = [pltpu.roll(packed, (lane_of - first - q) % 128, 1) for q in range(count)]
    return jnp.where(keep, jnp.concatenate(out, 0), 0.0)


def step(
    sizes, e_hbm, h_hbm, ef_hbm, ec_hbm, hc_hbm, dft_hbm, modes_hbm,
    mask_hbm, omega_hbm, pidx_hbm, powner_hbm, mon_hbm,
    en, hn, dn, rows, aux,
    ef, ec, hc, modes, mask_ref, omega_ref, pidx_ref, powner_ref, mon_ref,
    hx_in, hy_in, hz_in, ex_in, ey_in, ez_in, hy_out, ey_out, mine,
    cx_in, cz_in, mz_in, cx_out,
    load_sems, h_send, h_recv, e_send, e_recv, c_send, c_recv, all_send, all_recv,
    near_sems, far_sems, known_sems,
):
    n_gx, n_gy, n_gz = sizes
    n = n_gx * n_gy * n_gz
    kinds = rows.shape[1]
    a, b, c = lax.axis_index("gx"), lax.axis_index("gy"), lax.axis_index("gz")
    stride_x, stride_y = n_gy * n_gz, n_gz
    me = a * stride_x + b * stride_y + c
    nx, nz, ny = ec.shape
    zt = nz // 8

    lines = [(a, n_gx, stride_x), (b, n_gy, stride_y), (c, n_gz, 1)]

    def signal(sem, dev):
        pl.semaphore_signal(sem, inc=1, device_id=dev, device_id_type=pl.DeviceIdType.LOGICAL)

    def tell(line, sem):
        at, size, stride = line
        for k in range(1, size):
            signal(sem, me + (lax.rem(at + k, size) - at) * stride)

    def tell_line():
        for k in range(1, n_gz):
            pl.when(c + k < n_gz)(functools.partial(signal, known_sems.at[1], me + k))
            pl.when(c >= k)(functools.partial(signal, known_sems.at[3], me - k))

    def far_upper(axis):
        at, size, _ = lines[axis]
        if size > 2:

            @pl.when(at < size - 2)
            def _():
                pl.semaphore_wait(far_sems.at[axis], size - 2 - at)

    barrier = pltpu.get_barrier_semaphore()
    loads = [
        pltpu.make_async_copy(src, dst, load_sems.at[i])
        for i, (src, dst) in enumerate(
            [(h_hbm, hn), (e_hbm, en), (ec_hbm, ec), (modes_hbm, modes), (hc_hbm, hc), (ef_hbm, ef), (dft_hbm, dn),
             (mask_hbm, mask_ref), (omega_hbm, omega_ref), (pidx_hbm, pidx_ref), (powner_hbm, powner_ref), (mon_hbm, mon_ref)]
        )
    ]
    first = pltpu.make_async_copy(ec_hbm.at[0], cx_out, load_sems.at[12])
    first.start()
    for at, size, stride in lines:
        for k in range(1, size):
            pl.when(at + k < size)(functools.partial(signal, barrier, me + k * stride))

    def remote(src, dst, send, recv, dev):
        return pltpu.make_async_remote_copy(
            src_ref=src, dst_ref=dst, send_sem=send, recv_sem=recv,
            device_id=dev, device_id_type=pl.DeviceIdType.LOGICAL,
        )

    up = [(a < n_gx - 1, stride_x), (b < n_gy - 1, stride_y), (c < n_gz - 1, 1)]
    down = [(a > 0, stride_x), (b > 0, stride_y), (c > 0, 1)]
    h_copies = [
        remote(src, dst, h_send.at[i], h_recv.at[i], jnp.where(up[i][0], me + up[i][1], 0))
        for i, (src, dst) in enumerate(
            [(hn.at[1:3, nx - 1], hx_in), (hy_out, hy_in), (hn.at[0:2, :, nz - 1], hz_in)]
        )
    ]
    e_copies = [
        remote(src, dst, e_send.at[i], e_recv.at[i], jnp.where(down[i][0], me - down[i][1], 0))
        for i, (src, dst) in enumerate(
            [(en.at[1:3, 0], ex_in), (ey_out, ey_in), (en.at[0:2, :, 0], ez_in)]
        )
    ]

    c_copies = [
        (i, remote(src, dst, c_send.at[k], c_recv.at[k], jnp.where(down[i][0], me - down[i][1], 0)))
        for k, (i, src, dst) in enumerate(
            [(0, cx_out, cx_in), (2, ec_hbm.at[:, 0], cz_in), (2, modes_hbm.at[:, 0, 0], mz_in)]
        )
    ]

    row = lax.broadcasted_iota(jnp.int32, (nz, ny), 0)
    lane = lax.broadcasted_iota(jnp.int32, (nz, ny), 1)
    lane8 = lax.broadcasted_iota(jnp.int32, (8, 128), 1)
    group = 128 // NP

    sub8 = lax.broadcasted_iota(jnp.int32, (8, 128), 0)

    @pl.when(me > 0)
    def _():
        pl.semaphore_wait(barrier, a + b + c)

    for i, copy in c_copies[1:]:
        pl.when(down[i][0])(copy.start)
    for axis, (at, size, stride) in enumerate(lines):
        for k in range(1, size if axis else 2):
            sem = (far_sems if k > 1 else near_sems).at[axis]
            pl.when(at >= k)(functools.partial(signal, sem, me - k * stride))
    first.wait()
    pl.when(down[0][0])(c_copies[0][1].start)

    for i in (0, 9, 2, 1, 3):
        loads[i].start()
    for i in (7, 8, 10, 11, 4, 5, 6):
        loads[i].start()

    loads[0].wait()
    hy_out[...] = pack_lane(
        [hn[comp, x] for comp in (0, 2) for x in range(nx)], ny - 1, lane8
    )
    for i in (2, 0, 1):

        @pl.when(up[i][0])
        def _(i=i):
            pl.semaphore_wait(near_sems.at[i], 1)
            h_copies[i].start()

    far_upper(1)
    tell(lines[1], known_sems.at[0])

    for i in (7, 8, 9, 10, 11):
        loads[i].wait()
    angle_rows = jnp.zeros((8, 128), jnp.float32)
    angle_lanes = jnp.zeros((8, 128), jnp.float32)
    for f in range(NF):
        angle_rows = jnp.where(sub8 == f, omega_ref[f], angle_rows)
        angle_lanes = jnp.where((lane8 == f) | (lane8 == f + NF), omega_ref[f], angle_lanes)
    cosines, sines = jnp.cos(angle_rows), -jnp.sin(angle_rows)
    phase_lanes = jnp.where(lane8 < NF, jnp.cos(angle_lanes), -jnp.sin(angle_lanes))
    weight = jnp.zeros((8, 128), jnp.float32)
    for k in range(ny // BY):
        weight = jnp.where(lane8 // BY == k, mask_ref[0, 0, k].astype(jnp.float32), weight)
    weight = jnp.concatenate([weight] * zt, 0)
    port = lax.broadcasted_iota(jnp.int32, (1, 128), 1) // group
    owned = jnp.zeros((1, 128), jnp.float32)
    for p in range(NP):
        owned = jnp.where(port == p, (powner_ref[p] == me).astype(jnp.float32), owned)
    aux[0:1] = owned
    aux[1:2] = phase_lanes[0:1]
    aux[2:3, : 2 * NF] = mon_ref[...]

    for i in (1, 2, 3):
        loads[i].wait()

    ports = []
    for p in range(NP):
        x_of = pidx_ref[p] - a * nx
        ports.append(((x_of >= 0) & (x_of < nx), x_of == nx, jnp.clip(x_of, 0, nx - 1)))

    def low(plane, axis):
        first = (row if axis == 0 else lane) == 0
        return plane - jnp.where(first, 0.0, pltpu.roll(plane, 1, axis))

    for x in range(nx):
        h0, h1, h2 = hn[0, x], hn[1, x], hn[2, x]
        d1 = h1 - hn[1, x - 1] if x else h1
        d2 = h2 - hn[2, x - 1] if x else h2
        coef = ec[x]
        en[0, x] = en[0, x] - coef * (low(h2, 1) - low(h1, 0))
        en[1, x] = en[1, x] - coef * (low(h0, 0) - d2)
        en[2, x] = en[2, x] - coef * (d1 - low(h0, 1))

    partial = []
    for p, (inside, _, at) in enumerate(ports):
        both = modes[p, 0] * en[1, at] + modes[p, 1] * en[2, at]
        partial.append(jnp.where(inside, functools.reduce(jnp.add, tiles(both)), 0.0))

    def column(planes, lane_of):
        packed = jnp.zeros((8, 128), jnp.float32)
        for p, plane in enumerate(planes):
            for q, tile in enumerate(tiles(plane)):
                to = p * group + q
                packed = jnp.where(lane8 == to, pltpu.roll(tile, (to - lane_of) % 128, 1), packed)
        packed = pltpu.roll(packed, 0, 1, stride=zt, stride_axis=0)
        return jnp.sum(packed, axis=0, keepdims=True)

    columns = []
    if n_gy > 1:
        below = [jnp.where(inside, -hn[0, at], 0.0) for inside, _, at in ports]
        above = [modes[p, 1] * ec[at] for p, (_, _, at) in enumerate(ports)]
        if n_gy == 2:
            edge = jnp.broadcast_to(b == 0, (nz, ny))
            both = [jnp.where(edge, pltpu.roll(u, 1, 1), v) for u, v in zip(below, above)]
            columns = [column(both, 0)]
        else:
            columns = [column(below, ny - 1), column(above, 0)]

    x_parts = [
        jnp.where(over, modes[p, 1] * hn[1, nx - 1] - modes[p, 0] * hn[2, nx - 1], 0.0)
        for p, (_, over, _) in enumerate(ports)
    ]
    z_parts = [jnp.where(inside, hn[0, at, nz - 1 : nz], 0.0) for inside, _, at in ports]

    if n_gy > 1:
        pl.semaphore_wait(known_sems.at[0], n_gy - 1)
    far_upper(2)
    tell_line()

    for (i, copy), landing in zip(c_copies, (cx_in, cz_in, mz_in)):
        pl.when(up[i][0])(copy.wait_recv)

        @pl.when(jnp.logical_not(up[i][0]))
        def _(landing=landing):
            landing[...] = jnp.zeros_like(landing)

    share = jnp.zeros((8, 128), jnp.float32)
    for p, (_, _, at) in enumerate(ports):
        x_part = functools.reduce(jnp.add, tiles(cx_in[...] * x_parts[p]))
        z_part = mz_in[p : p + 1] * cz_in[pl.ds(at, 1)] * z_parts[p]
        total = partial[p] + x_part + jnp.where(sub8 == 0, z_part, 0.0)
        width = 128
        while width > group:
            width //= 2
            total = total + pltpu.roll(total, width, 1)
        share = jnp.where(lane8 // group == p, total, share)
    mine[0, 0:1] = jnp.sum(share, axis=0, keepdims=True)
    for k, vector in enumerate(columns):
        mine[0, k + 1 : k + 2] = vector
    rows[pl.ds(me, 1)] = mine[...]

    @pl.when(c > 0)
    def _():
        pl.semaphore_wait(known_sems.at[1], c)

    def send_rows(plane, part):
        def send_row(k, _):
            to = plane * stride_x + k
            near = k % n_gz <= c
            wanted = {"near": near, "far": jnp.logical_not(near), "all": True}[part]
            pl.when((to != me) & wanted)(remote(mine.at[0], rows.at[me], all_send, all_recv, to).start)
            return 0

        lax.fori_loop(0, stride_x, send_row, 0, unroll=n <= UNROLL)

    for plane in range(n_gx):
        pl.when(plane <= a)(functools.partial(send_rows, plane, "near"))

    @pl.when(c < n_gz - 1)
    def _():
        pl.semaphore_wait(known_sems.at[3], n_gz - 1 - c)

    for k in range(1, n_gx):
        pl.when(a >= k)(functools.partial(signal, known_sems.at[2], me - k * stride_x))

    for plane in range(n_gx):
        pl.when(plane <= a)(functools.partial(send_rows, plane, "far"))

    for i, landing in enumerate((hx_in, hy_in, hz_in)):
        pl.when(down[i][0])(h_copies[i].wait_recv)

        @pl.when(jnp.logical_not(down[i][0]))
        def _(landing=landing):
            landing[...] = jnp.zeros_like(landing)

    packed = hy_in[...]
    for x in range(nx):
        coef = ec[x]
        y0 = unpack_lane(packed, x * zt, zt, 0, lane == 0)
        y2 = unpack_lane(packed, (nx + x) * zt, zt, 0, lane == 0)
        z0 = jnp.where(sub8 == 0, hz_in[0, x : x + 1, :], 0.0)
        z1 = jnp.where(sub8 == 0, hz_in[1, x : x + 1, :], 0.0)
        rest = jnp.zeros((nz - 8, ny), jnp.float32)
        z0, z1 = jnp.concatenate([z0, rest], 0), jnp.concatenate([z1, rest], 0)
        add0, add1, add2 = y2 - z1, z0, -y0
        if x == 0:
            add1 = add1 - hx_in[1]
            add2 = add2 + hx_in[0]
        en[0, x] = en[0, x] + coef * add0
        en[1, x] = en[1, x] + coef * add1
        en[2, x] = en[2, x] + coef * add2
        if x == 0:
            pl.when(down[0][0])(e_copies[0].start)

    pl.when(down[2][0])(e_copies[2].start)
    ey_out[...] = pack_lane([en[comp, x] for comp in (0, 2) for x in range(nx)], 0, lane8)
    pl.when(down[1][0])(e_copies[1].start)

    for i in range(3):
        pl.when(up[i][0])(h_copies[i].wait_send)
    loads[4].wait()

    def high(plane, axis):
        last = (row == nz - 1) if axis == 0 else (lane == ny - 1)
        return jnp.where(last, 0.0, pltpu.roll(plane, plane.shape[axis] - 1, axis)) - plane

    for x in range(nx):
        e0, e1, e2 = en[0, x], en[1, x], en[2, x]
        d1 = en[1, x + 1] - e1 if x < nx - 1 else -e1
        d2 = en[2, x + 1] - e2 if x < nx - 1 else -e2
        coef = hc[x]
        hn[0, x] = hn[0, x] + coef * (high(e2, 1) - high(e1, 0))
        hn[1, x] = hn[1, x] + coef * (high(e0, 0) - d2)
        hn[2, x] = hn[2, x] + coef * (d1 - high(e0, 1))

    loads[5].wait()
    loads[6].wait()
    for x in range(nx):
        product = weight * (ef[0, x] * en[0, x] + ef[1, x] * en[1, x] + ef[2, x] * en[2, x])
        for f in range(NF):
            dn[f, x] = dn[f, x] + cosines[f : f + 1] * product
            dn[NF + f, x] = dn[NF + f, x] + sines[f : f + 1] * product

    @pl.when(a < n_gx - 1)
    def _():
        pl.semaphore_wait(known_sems.at[2], n_gx - 1 - a)

    for plane in range(n_gx - 1, 0, -1):
        pl.when(plane > a)(functools.partial(send_rows, plane, "all"))

    for i, landing in enumerate((ex_in, ey_in, ez_in)):
        pl.when(up[i][0])(e_copies[i].wait_recv)

        @pl.when(jnp.logical_not(up[i][0]))
        def _(landing=landing):
            landing[...] = jnp.zeros_like(landing)

    packed = ey_in[...]
    for x in range(nx):
        coef = hc[x]
        y0 = unpack_lane(packed, x * zt, zt, ny - 1, lane == ny - 1)
        y2 = unpack_lane(packed, (nx + x) * zt, zt, ny - 1, lane == ny - 1)
        z0 = jnp.where(sub8 == 7, ez_in[0, x : x + 1, :], 0.0)
        z1 = jnp.where(sub8 == 7, ez_in[1, x : x + 1, :], 0.0)
        rest = jnp.zeros((nz - 8, ny), jnp.float32)
        z0, z1 = jnp.concatenate([rest, z0], 0), jnp.concatenate([rest, z1], 0)
        add0, add1, add2 = y2 - z1, z0, -y0
        if x == nx - 1:
            add1 = add1 - ex_in[1]
            add2 = add2 + ex_in[0]
        hn[0, x] = hn[0, x] + coef * add0
        hn[1, x] = hn[1, x] + coef * add1
        hn[2, x] = hn[2, x] + coef * add2
    for i in range(3):
        pl.when(down[i][0])(e_copies[i].wait_send)

    for i, copy in c_copies:
        pl.when(down[i][0])(copy.wait_send)

    others = rows.at[pl.ds(0, n - 1)]
    remote(others, others, all_send, all_recv, me).wait()


def write_out(sizes, en, hn, dn, rows, aux, en_out, hn_out, dn_out, mon_out, mon, sems):
    parts = 4
    size = dn.shape[0] // parts
    pairs = [(dn.at[pl.ds(i * size, size)], dn_out.at[pl.ds(i * size, size)]) for i in range(parts)]
    pairs += [(en, en_out), (hn, hn_out), (mon, mon_out)]
    copies = [pltpu.make_async_copy(src, dst, sems.at[i]) for i, (src, dst) in enumerate(pairs)]
    for copy in copies[:-1]:
        copy.start()
    kinds = rows.shape[1]
    n_gy = sizes[1]
    intersection = jnp.sum(rows[:, 0:1], axis=0)
    if n_gy > 1:
        grid = (*sizes, 1, 128)
        lower = rows[:, 1:2].reshape(grid)[:, : n_gy - 1]
        upper = rows[:, kinds - 1 : kinds].reshape(grid)[:, 1:]
        intersection = intersection + jnp.sum(lower * upper, axis=(0, 1, 2))
    total = jnp.sum(aux[0:1] * intersection, axis=1, keepdims=True)
    mon[...] = aux[2:3, : 2 * NF] + total * aux[1:2, : 2 * NF]
    copies[-1].start()
    for copy in copies:
        copy.wait()


def body(sizes, e_field, h_field, e_forward, e_coeff, h_coeff, dft_acc, design_mask,
         omega_t, port_index, port_owner, port_modes, monitor_acc):
    nx, nz, ny = e_coeff.shape
    n = sizes[0] * sizes[1] * sizes[2]
    kinds = min(sizes[1], 3)
    f32 = jnp.float32
    hbm = pl.BlockSpec(memory_space=pltpu.HBM)
    vmem = pl.BlockSpec(memory_space=pltpu.VMEM)
    far = lambda x: pltpu.with_memory_space_constraint(x, pltpu.HBM)
    held = pl.pallas_call(
        functools.partial(step, sizes),
        out_shape=[
            pltpu.VMEM(e_field.shape, f32),
            pltpu.VMEM(h_field.shape, f32),
            pltpu.VMEM(dft_acc.shape, f32),
            pltpu.VMEM((n, kinds, 128), f32),
            pltpu.VMEM((3, 128), f32),
        ],
        in_specs=[hbm] * 12,
        out_specs=[vmem] * 5,
        scratch_shapes=[
            pltpu.VMEM(e_forward.shape, f32),
            pltpu.VMEM(e_coeff.shape, f32),
            pltpu.VMEM(h_coeff.shape, f32),
            pltpu.VMEM(port_modes.shape, f32),
            pltpu.SMEM(design_mask.shape, jnp.int32),
            pltpu.SMEM(omega_t.shape, f32),
            pltpu.SMEM(port_index.shape, jnp.int32),
            pltpu.SMEM(port_owner.shape, jnp.int32),
            pltpu.VMEM(monitor_acc.shape, f32),
            pltpu.VMEM((2, nz, ny), f32),
            pltpu.VMEM((8, 128), f32),
            pltpu.VMEM((2, nx, ny), f32),
            pltpu.VMEM((2, nz, ny), f32),
            pltpu.VMEM((8, 128), f32),
            pltpu.VMEM((2, nx, ny), f32),
            pltpu.VMEM((8, 128), f32),
            pltpu.VMEM((8, 128), f32),
            pltpu.VMEM((1, kinds, 128), f32),
            pltpu.VMEM((nz, ny), f32),
            pltpu.VMEM((nx, ny), f32),
            pltpu.VMEM((NP, ny), f32),
            pltpu.VMEM((nz, ny), f32),
            pltpu.SemaphoreType.DMA((13,)),
            pltpu.SemaphoreType.DMA((3,)),
            pltpu.SemaphoreType.DMA((3,)),
            pltpu.SemaphoreType.DMA((3,)),
            pltpu.SemaphoreType.DMA((3,)),
            pltpu.SemaphoreType.DMA((3,)),
            pltpu.SemaphoreType.DMA((3,)),
            pltpu.SemaphoreType.DMA,
            pltpu.SemaphoreType.DMA,
            pltpu.SemaphoreType.REGULAR((3,)),
            pltpu.SemaphoreType.REGULAR((3,)),
            pltpu.SemaphoreType.REGULAR((4,)),
        ],
        compiler_params=pltpu.CompilerParams(
            collective_id=0, has_side_effects=True, vmem_limit_bytes=24 * 2**20
        ),
        name="yee_step",
    )(*map(far, (e_field, h_field, e_forward, e_coeff, h_coeff, dft_acc, port_modes,
      design_mask, omega_t, port_index, port_owner, monitor_acc)))
    shape = lambda x: jax.ShapeDtypeStruct(x.shape, f32)
    return pl.pallas_call(
        functools.partial(write_out, sizes),
        out_shape=[shape(x) for x in (e_field, h_field, dft_acc, monitor_acc)],
        in_specs=[vmem] * 5,
        out_specs=[hbm] * 4,
        scratch_shapes=[pltpu.VMEM(monitor_acc.shape, f32), pltpu.SemaphoreType.DMA((7,))],
        name="write_out",
    )(*[pltpu.with_memory_space_constraint(x, pltpu.VMEM) for x in held])


def solution(mesh):
    grid = P(None, "gx", "gz", "gy")
    brick = P("gx", "gz", "gy")
    own = P(("gx", "gy", "gz"), None)
    sizes = tuple(mesh.shape[axis] for axis in ("gx", "gy", "gz"))
    in_specs = (grid, grid, grid, brick, brick, grid, brick, P(), P(), P(),
                P(None, None, "gz", "gy"), own)
    return jax.shard_map(
        functools.partial(body, sizes), mesh=mesh, in_specs=in_specs,
        out_specs=(grid, grid, grid, own), check_vma=False,
    )
```

```python
import functools

import jax
import jax.numpy as jnp
from jax import lax
from jax.experimental import pallas as pl
from jax.experimental.pallas import tpu as pltpu
from jax.sharding import PartitionSpec as P

BY = 8
NF = 8
NP = 4
UNROLL = 32


def tiles(plane):
    return [plane[8 * q : 8 * q + 8] for q in range(plane.shape[0] // 8)]


def pack_lane(fields, lane_of, lane):
    packed = jnp.zeros((8, 128), jnp.float32)
    k = 0
    for plane in fields:
        for tile in tiles(plane):
            moved = pltpu.roll(tile, (k - lane_of) % 128, 1)
            packed = jnp.where(lane == k, moved, packed)
            k += 1
    return packed


def unpack_lane(packed, first, count, lane_of, keep):
    out = [pltpu.roll(packed, (lane_of - first - q) % 128, 1) for q in range(count)]
    return jnp.where(keep, jnp.concatenate(out, 0), 0.0)


def step(
    sizes, e_hbm, h_hbm, ef_hbm, ec_hbm, hc_hbm, dft_hbm, modes_hbm,
    mask_hbm, omega_hbm, pidx_hbm, powner_hbm, mon_hbm,
    en, hn, dn, rows, aux,
    ef, ec, hc, modes, mask_ref, omega_ref, pidx_ref, powner_ref, mon_ref,
    hx_in, hy_in, hz_in, ex_in, ey_in, ez_in, hy_out, ey_out, mine,
    cx_in, cz_in, mz_in, cx_out,
    load_sems, h_send, h_recv, e_send, e_recv, c_send, c_recv, all_send, all_recv,
    near_sems, far_sems, known_sems,
):
    n_gx, n_gy, n_gz = sizes
    n = n_gx * n_gy * n_gz
    kinds = rows.shape[1]
    a, b, c = lax.axis_index("gx"), lax.axis_index("gy"), lax.axis_index("gz")
    stride_x, stride_y = n_gy * n_gz, n_gz
    me = a * stride_x + b * stride_y + c
    nx, nz, ny = ec.shape
    zt = nz // 8

    lines = [(a, n_gx, stride_x), (b, n_gy, stride_y), (c, n_gz, 1)]

    def signal(sem, dev):
        pl.semaphore_signal(sem, inc=1, device_id=dev, device_id_type=pl.DeviceIdType.LOGICAL)

    def tell(line, sem):
        at, size, stride = line
        for k in range(1, size):
            signal(sem, me + (lax.rem(at + k, size) - at) * stride)

    def tell_line():
        for k in range(1, n_gz):
            pl.when(c + k < n_gz)(functools.partial(signal, known_sems.at[1], me + k))
            pl.when(c >= k)(functools.partial(signal, known_sems.at[3], me - k))

    def far_upper(axis):
        at, size, _ = lines[axis]
        if size > 2:

            @pl.when(at < size - 2)
            def _():
                pl.semaphore_wait(far_sems.at[axis], size - 2 - at)

    barrier = pltpu.get_barrier_semaphore()
    loads = [
        pltpu.make_async_copy(src, dst, load_sems.at[i])
        for i, (src, dst) in enumerate(
            [(h_hbm, hn), (e_hbm, en), (ec_hbm, ec), (modes_hbm, modes), (hc_hbm, hc), (ef_hbm, ef), (dft_hbm, dn),
             (mask_hbm, mask_ref), (omega_hbm, omega_ref), (pidx_hbm, pidx_ref), (powner_hbm, powner_ref), (mon_hbm, mon_ref)]
        )
    ]
    first = pltpu.make_async_copy(ec_hbm.at[0], cx_out, load_sems.at[12])
    first.start()
    for at, size, stride in lines:
        for k in range(1, size):
            pl.when(at + k < size)(functools.partial(signal, barrier, me + k * stride))

    def remote(src, dst, send, recv, dev):
        return pltpu.make_async_remote_copy(
            src_ref=src, dst_ref=dst, send_sem=send, recv_sem=recv,
            device_id=dev, device_id_type=pl.DeviceIdType.LOGICAL,
        )

    up = [(a < n_gx - 1, stride_x), (b < n_gy - 1, stride_y), (c < n_gz - 1, 1)]
    down = [(a > 0, stride_x), (b > 0, stride_y), (c > 0, 1)]
    h_copies = [
        remote(src, dst, h_send.at[i], h_recv.at[i], jnp.where(up[i][0], me + up[i][1], 0))
        for i, (src, dst) in enumerate(
            [(hn.at[1:3, nx - 1], hx_in), (hy_out, hy_in), (hn.at[0:2, :, nz - 1], hz_in)]
        )
    ]
    e_copies = [
        remote(src, dst, e_send.at[i], e_recv.at[i], jnp.where(down[i][0], me - down[i][1], 0))
        for i, (src, dst) in enumerate(
            [(en.at[1:3, 0], ex_in), (ey_out, ey_in), (en.at[0:2, :, 0], ez_in)]
        )
    ]

    c_copies = [
        (i, remote(src, dst, c_send.at[k], c_recv.at[k], jnp.where(down[i][0], me - down[i][1], 0)))
        for k, (i, src, dst) in enumerate(
            [(0, cx_out, cx_in), (2, ec_hbm.at[:, 0], cz_in), (2, modes_hbm.at[:, 0, 0], mz_in)]
        )
    ]

    row = lax.broadcasted_iota(jnp.int32, (nz, ny), 0)
    lane = lax.broadcasted_iota(jnp.int32, (nz, ny), 1)
    lane8 = lax.broadcasted_iota(jnp.int32, (8, 128), 1)
    group = 128 // NP

    sub8 = lax.broadcasted_iota(jnp.int32, (8, 128), 0)

    @pl.when(me > 0)
    def _():
        pl.semaphore_wait(barrier, a + b + c)

    for i, copy in c_copies[1:]:
        pl.when(down[i][0])(copy.start)
    for axis, (at, size, stride) in enumerate(lines):
        for k in range(1, size if axis else 2):
            sem = (far_sems if k > 1 else near_sems).at[axis]
            pl.when(at >= k)(functools.partial(signal, sem, me - k * stride))
    first.wait()
    pl.when(down[0][0])(c_copies[0][1].start)

    for i in (0, 9, 2, 1, 3):
        loads[i].start()
    for i in (7, 8, 10, 11, 4, 5, 6):
        loads[i].start()

    loads[0].wait()
    hy_out[...] = pack_lane(
        [hn[comp, x] for comp in (0, 2) for x in range(nx)], ny - 1, lane8
    )
    for i in (2, 0, 1):

        @pl.when(up[i][0])
        def _(i=i):
            pl.semaphore_wait(near_sems.at[i], 1)
            h_copies[i].start()

    far_upper(1)
    tell(lines[1], known_sems.at[0])

    for i in (7, 8, 9, 10, 11):
        loads[i].wait()
    angle_rows = jnp.zeros((8, 128), jnp.float32)
    angle_lanes = jnp.zeros((8, 128), jnp.float32)
    for f in range(NF):
        angle_rows = jnp.where(sub8 == f, omega_ref[f], angle_rows)
        angle_lanes = jnp.where((lane8 == f) | (lane8 == f + NF), omega_ref[f], angle_lanes)
    cosines, sines = jnp.cos(angle_rows), -jnp.sin(angle_rows)
    phase_lanes = jnp.where(lane8 < NF, jnp.cos(angle_lanes), -jnp.sin(angle_lanes))
    weight = jnp.zeros((8, 128), jnp.float32)
    for k in range(ny // BY):
        weight = jnp.where(lane8 // BY == k, mask_ref[0, 0, k].astype(jnp.float32), weight)
    weight = jnp.concatenate([weight] * zt, 0)
    port = lax.broadcasted_iota(jnp.int32, (1, 128), 1) // group
    owned = jnp.zeros((1, 128), jnp.float32)
    for p in range(NP):
        owned = jnp.where(port == p, (powner_ref[p] == me).astype(jnp.float32), owned)
    aux[0:1] = owned
    aux[1:2] = phase_lanes[0:1]
    aux[2:3, : 2 * NF] = mon_ref[...]

    for i in (1, 2, 3):
        loads[i].wait()

    ports = []
    for p in range(NP):
        x_of = pidx_ref[p] - a * nx
        ports.append(((x_of >= 0) & (x_of < nx), x_of == nx, jnp.clip(x_of, 0, nx - 1)))

    def low(plane, axis):
        first = (row if axis == 0 else lane) == 0
        return plane - jnp.where(first, 0.0, pltpu.roll(plane, 1, axis))

    for x in range(nx):
        h0, h1, h2 = hn[0, x], hn[1, x], hn[2, x]
        d1 = h1 - hn[1, x - 1] if x else h1
        d2 = h2 - hn[2, x - 1] if x else h2
        coef = ec[x]
        en[0, x] = en[0, x] - coef * (low(h2, 1) - low(h1, 0))
        en[1, x] = en[1, x] - coef * (low(h0, 0) - d2)
        en[2, x] = en[2, x] - coef * (d1 - low(h0, 1))

    partial = []
    for p, (inside, _, at) in enumerate(ports):
        both = modes[p, 0] * en[1, at] + modes[p, 1] * en[2, at]
        partial.append(jnp.where(inside, functools.reduce(jnp.add, tiles(both)), 0.0))

    def column(planes, lane_of):
        packed = jnp.zeros((8, 128), jnp.float32)
        for p, plane in enumerate(planes):
            for q, tile in enumerate(tiles(plane)):
                to = p * group + q
                packed = jnp.where(lane8 == to, pltpu.roll(tile, (to - lane_of) % 128, 1), packed)
        packed = pltpu.roll(packed, 0, 1, stride=zt, stride_axis=0)
        return jnp.sum(packed, axis=0, keepdims=True)

    columns = []
    if n_gy > 1:
        below = [jnp.where(inside, -hn[0, at], 0.0) for inside, _, at in ports]
        above = [modes[p, 1] * ec[at] for p, (_, _, at) in enumerate(ports)]
        if n_gy == 2:
            edge = jnp.broadcast_to(b == 0, (nz, ny))
            both = [jnp.where(edge, pltpu.roll(u, 1, 1), v) for u, v in zip(below, above)]
            columns = [column(both, 0)]
        else:
            columns = [column(below, ny - 1), column(above, 0)]

    x_parts = [
        jnp.where(over, modes[p, 1] * hn[1, nx - 1] - modes[p, 0] * hn[2, nx - 1], 0.0)
        for p, (_, over, _) in enumerate(ports)
    ]
    z_parts = [jnp.where(inside, hn[0, at, nz - 1 : nz], 0.0) for inside, _, at in ports]

    if n_gy > 1:
        pl.semaphore_wait(known_sems.at[0], n_gy - 1)
    far_upper(2)
    tell_line()

    for (i, copy), landing in zip(c_copies, (cx_in, cz_in, mz_in)):
        pl.when(up[i][0])(copy.wait_recv)

        @pl.when(jnp.logical_not(up[i][0]))
        def _(landing=landing):
            landing[...] = jnp.zeros_like(landing)

    share = jnp.zeros((8, 128), jnp.float32)
    for p, (_, _, at) in enumerate(ports):
        x_part = functools.reduce(jnp.add, tiles(cx_in[...] * x_parts[p]))
        z_part = mz_in[p : p + 1] * cz_in[pl.ds(at, 1)] * z_parts[p]
        total = partial[p] + x_part + jnp.where(sub8 == 0, z_part, 0.0)
        width = 128
        while width > group:
            width //= 2
            total = total + pltpu.roll(total, width, 1)
        share = jnp.where(lane8 // group == p, total, share)
    mine[0, 0:1] = jnp.sum(share, axis=0, keepdims=True)
    for k, vector in enumerate(columns):
        mine[0, k + 1 : k + 2] = vector
    rows[pl.ds(me, 1)] = mine[...]

    @pl.when(c > 0)
    def _():
        pl.semaphore_wait(known_sems.at[1], c)

    def send_rows(plane, part):
        def send_row(k, _):
            to = plane * stride_x + k
            near = k % n_gz <= c
            wanted = {"near": near, "far": jnp.logical_not(near), "all": True}[part]
            pl.when((to != me) & wanted)(remote(mine.at[0], rows.at[me], all_send, all_recv, to).start)
            return 0

        lax.fori_loop(0, stride_x, send_row, 0, unroll=n <= UNROLL)

    for plane in range(n_gx):
        pl.when(plane <= a)(functools.partial(send_rows, plane, "near"))

    @pl.when(c < n_gz - 1)
    def _():
        pl.semaphore_wait(known_sems.at[3], n_gz - 1 - c)

    for k in range(1, n_gx):
        pl.when(a >= k)(functools.partial(signal, known_sems.at[2], me - k * stride_x))

    for plane in range(n_gx):
        pl.when(plane <= a)(functools.partial(send_rows, plane, "far"))

    for i, landing in enumerate((hx_in, hy_in, hz_in)):
        pl.when(down[i][0])(h_copies[i].wait_recv)

        @pl.when(jnp.logical_not(down[i][0]))
        def _(landing=landing):
            landing[...] = jnp.zeros_like(landing)

    packed = hy_in[...]
    for x in range(nx):
        coef = ec[x]
        y0 = unpack_lane(packed, x * zt, zt, 0, lane == 0)
        y2 = unpack_lane(packed, (nx + x) * zt, zt, 0, lane == 0)
        z0 = jnp.where(sub8 == 0, hz_in[0, x : x + 1, :], 0.0)
        z1 = jnp.where(sub8 == 0, hz_in[1, x : x + 1, :], 0.0)
        rest = jnp.zeros((nz - 8, ny), jnp.float32)
        z0, z1 = jnp.concatenate([z0, rest], 0), jnp.concatenate([z1, rest], 0)
        add0, add1, add2 = y2 - z1, z0, -y0
        if x == 0:
            add1 = add1 - hx_in[1]
            add2 = add2 + hx_in[0]
        en[0, x] = en[0, x] + coef * add0
        en[1, x] = en[1, x] + coef * add1
        en[2, x] = en[2, x] + coef * add2
        if x == 0:
            pl.when(down[0][0])(e_copies[0].start)

    pl.when(down[2][0])(e_copies[2].start)
    ey_out[...] = pack_lane([en[comp, x] for comp in (0, 2) for x in range(nx)], 0, lane8)
    pl.when(down[1][0])(e_copies[1].start)

    for i in range(3):
        pl.when(up[i][0])(h_copies[i].wait_send)
    loads[4].wait()

    def high(plane, axis):
        last = (row == nz - 1) if axis == 0 else (lane == ny - 1)
        return jnp.where(last, 0.0, pltpu.roll(plane, plane.shape[axis] - 1, axis)) - plane

    for x in range(nx):
        e0, e1, e2 = en[0, x], en[1, x], en[2, x]
        d1 = en[1, x + 1] - e1 if x < nx - 1 else -e1
        d2 = en[2, x + 1] - e2 if x < nx - 1 else -e2
        coef = hc[x]
        hn[0, x] = hn[0, x] + coef * (high(e2, 1) - high(e1, 0))
        hn[1, x] = hn[1, x] + coef * (high(e0, 0) - d2)
        hn[2, x] = hn[2, x] + coef * (d1 - high(e0, 1))

    @pl.when(a < n_gx - 1)
    def _():
        pl.semaphore_wait(known_sems.at[2], n_gx - 1 - a)

    for plane in range(n_gx - 1, 0, -1):
        pl.when(plane > a)(functools.partial(send_rows, plane, "all"))

    loads[5].wait()
    loads[6].wait()
    for x in range(nx):
        product = weight * (ef[0, x] * en[0, x] + ef[1, x] * en[1, x] + ef[2, x] * en[2, x])
        for f in range(NF):
            dn[f, x] = dn[f, x] + cosines[f : f + 1] * product
            dn[NF + f, x] = dn[NF + f, x] + sines[f : f + 1] * product

    for i, landing in enumerate((ex_in, ey_in, ez_in)):
        pl.when(up[i][0])(e_copies[i].wait_recv)

        @pl.when(jnp.logical_not(up[i][0]))
        def _(landing=landing):
            landing[...] = jnp.zeros_like(landing)

    packed = ey_in[...]
    for x in range(nx):
        coef = hc[x]
        y0 = unpack_lane(packed, x * zt, zt, ny - 1, lane == ny - 1)
        y2 = unpack_lane(packed, (nx + x) * zt, zt, ny - 1, lane == ny - 1)
        z0 = jnp.where(sub8 == 7, ez_in[0, x : x + 1, :], 0.0)
        z1 = jnp.where(sub8 == 7, ez_in[1, x : x + 1, :], 0.0)
        rest = jnp.zeros((nz - 8, ny), jnp.float32)
        z0, z1 = jnp.concatenate([rest, z0], 0), jnp.concatenate([rest, z1], 0)
        add0, add1, add2 = y2 - z1, z0, -y0
        if x == nx - 1:
            add1 = add1 - ex_in[1]
            add2 = add2 + ex_in[0]
        hn[0, x] = hn[0, x] + coef * add0
        hn[1, x] = hn[1, x] + coef * add1
        hn[2, x] = hn[2, x] + coef * add2
    for i in range(3):
        pl.when(down[i][0])(e_copies[i].wait_send)

    for i, copy in c_copies:
        pl.when(down[i][0])(copy.wait_send)

    others = rows.at[pl.ds(0, n - 1)]
    remote(others, others, all_send, all_recv, me).wait()


def write_out(sizes, en, hn, dn, rows, aux, en_out, hn_out, dn_out, mon_out, mon, sems):
    parts = 4
    size = dn.shape[0] // parts
    pairs = [(dn.at[pl.ds(i * size, size)], dn_out.at[pl.ds(i * size, size)]) for i in range(parts)]
    pairs += [(en, en_out), (hn, hn_out), (mon, mon_out)]
    copies = [pltpu.make_async_copy(src, dst, sems.at[i]) for i, (src, dst) in enumerate(pairs)]
    for copy in copies[:-1]:
        copy.start()
    kinds = rows.shape[1]
    n_gy = sizes[1]
    intersection = jnp.sum(rows[:, 0:1], axis=0)
    if n_gy > 1:
        grid = (*sizes, 1, 128)
        lower = rows[:, 1:2].reshape(grid)[:, : n_gy - 1]
        upper = rows[:, kinds - 1 : kinds].reshape(grid)[:, 1:]
        intersection = intersection + jnp.sum(lower * upper, axis=(0, 1, 2))
    total = jnp.sum(aux[0:1] * intersection, axis=1, keepdims=True)
    mon[...] = aux[2:3, : 2 * NF] + total * aux[1:2, : 2 * NF]
    copies[-1].start()
    for copy in copies:
        copy.wait()


def body(sizes, e_field, h_field, e_forward, e_coeff, h_coeff, dft_acc, design_mask,
         omega_t, port_index, port_owner, port_modes, monitor_acc):
    nx, nz, ny = e_coeff.shape
    n = sizes[0] * sizes[1] * sizes[2]
    kinds = min(sizes[1], 3)
    f32 = jnp.float32
    hbm = pl.BlockSpec(memory_space=pltpu.HBM)
    vmem = pl.BlockSpec(memory_space=pltpu.VMEM)
    far = lambda x: pltpu.with_memory_space_constraint(x, pltpu.HBM)
    held = pl.pallas_call(
        functools.partial(step, sizes),
        out_shape=[
            pltpu.VMEM(e_field.shape, f32),
            pltpu.VMEM(h_field.shape, f32),
            pltpu.VMEM(dft_acc.shape, f32),
            pltpu.VMEM((n, kinds, 128), f32),
            pltpu.VMEM((3, 128), f32),
        ],
        in_specs=[hbm] * 12,
        out_specs=[vmem] * 5,
        scratch_shapes=[
            pltpu.VMEM(e_forward.shape, f32),
            pltpu.VMEM(e_coeff.shape, f32),
            pltpu.VMEM(h_coeff.shape, f32),
            pltpu.VMEM(port_modes.shape, f32),
            pltpu.SMEM(design_mask.shape, jnp.int32),
            pltpu.SMEM(omega_t.shape, f32),
            pltpu.SMEM(port_index.shape, jnp.int32),
            pltpu.SMEM(port_owner.shape, jnp.int32),
            pltpu.VMEM(monitor_acc.shape, f32),
            pltpu.VMEM((2, nz, ny), f32),
            pltpu.VMEM((8, 128), f32),
            pltpu.VMEM((2, nx, ny), f32),
            pltpu.VMEM((2, nz, ny), f32),
            pltpu.VMEM((8, 128), f32),
            pltpu.VMEM((2, nx, ny), f32),
            pltpu.VMEM((8, 128), f32),
            pltpu.VMEM((8, 128), f32),
            pltpu.VMEM((1, kinds, 128), f32),
            pltpu.VMEM((nz, ny), f32),
            pltpu.VMEM((nx, ny), f32),
            pltpu.VMEM((NP, ny), f32),
            pltpu.VMEM((nz, ny), f32),
            pltpu.SemaphoreType.DMA((13,)),
            pltpu.SemaphoreType.DMA((3,)),
            pltpu.SemaphoreType.DMA((3,)),
            pltpu.SemaphoreType.DMA((3,)),
            pltpu.SemaphoreType.DMA((3,)),
            pltpu.SemaphoreType.DMA((3,)),
            pltpu.SemaphoreType.DMA((3,)),
            pltpu.SemaphoreType.DMA,
            pltpu.SemaphoreType.DMA,
            pltpu.SemaphoreType.REGULAR((3,)),
            pltpu.SemaphoreType.REGULAR((3,)),
            pltpu.SemaphoreType.REGULAR((4,)),
        ],
        compiler_params=pltpu.CompilerParams(
            collective_id=0, has_side_effects=True, vmem_limit_bytes=24 * 2**20
        ),
        name="yee_step",
    )(*map(far, (e_field, h_field, e_forward, e_coeff, h_coeff, dft_acc, port_modes,
      design_mask, omega_t, port_index, port_owner, monitor_acc)))
    shape = lambda x: jax.ShapeDtypeStruct(x.shape, f32)
    return pl.pallas_call(
        functools.partial(write_out, sizes),
        out_shape=[shape(x) for x in (e_field, h_field, dft_acc, monitor_acc)],
        in_specs=[vmem] * 5,
        out_specs=[hbm] * 4,
        scratch_shapes=[pltpu.VMEM(monitor_acc.shape, f32), pltpu.SemaphoreType.DMA((7,))],
        name="write_out",
    )(*[pltpu.with_memory_space_constraint(x, pltpu.VMEM) for x in held])


def solution(mesh):
    grid = P(None, "gx", "gz", "gy")
    brick = P("gx", "gz", "gy")
    own = P(("gx", "gy", "gz"), None)
    sizes = tuple(mesh.shape[axis] for axis in ("gx", "gy", "gz"))
    in_specs = (grid, grid, grid, brick, brick, grid, brick, P(), P(), P(),
                P(None, None, "gz", "gy"), own)
    return jax.shard_map(
        functools.partial(body, sizes), mesh=mesh, in_specs=in_specs,
        out_specs=(grid, grid, grid, own), check_vma=False,
    )
```
